32 devices in a mesh: gx: 4 (over y, x), gy: 8 (over z, core).
Axes of the slice: x: 2, y: 2, z: 4, core: 2. Of those that a mesh axis runs over, the one named last changes fastest.
Arguments:
- species: float32 [24, 64, 128, 128], P(None, 'gx', 'gy'), may hold values from -6 to 6
- diffusivity: float32 [64, 128, 128], P('gx', 'gy'), may hold values from 0.5 to 2
- lewis_number: float32 [24], replicated, may hold values from 0.5 to 2
- velocity: float32 [3, 64, 128, 128], P(None, 'gx', 'gy'), may hold values from -6 to 6
- layer_one: bfloat16 [1600, 24], replicated, may hold values from -1.25 to 1.25
- layer_two: bfloat16 [800, 1600], replicated, may hold values from -0.15625 to 0.15625
- layer_three: bfloat16 [400, 800], replicated, may hold values from -0.21875 to 0.21875
- layer_four: bfloat16 [24, 400], replicated, may hold values from -0.3125 to 0.3125
- heat_release: float32 [24], replicated, may hold values from -3 to 3
- react_index: int32 [4, 8, 4096], P('gx', 'gy'), may hold values from 0 to 32767, as said below
- react_count: int32 [4, 8], P('gx', 'gy'), may hold values from 1 to 4096, as said below
Outputs:
- species_out: float32 [24, 64, 128, 128], P(None, 'gx', 'gy')
- velocity_out: float32 [3, 64, 128, 128], P(None, 'gx', 'gy')
The draws below stay inside these ranges and needn't reach their ends.
Inputs may be any that keep to these rules, and one draw needn't show every extreme that they name: `react_index`: within each device's list the 4096 numbers are distinct cells of that device; slots from react_count on are padding. `react_count`: in every row of devices along gy the counts rounded up to whole blocks of 128 add up to at most 64, exactly that in some row; every such row has a device whose list is full.
All inputs are finite; a program needn't handle non-finite values.
Results may differ from the reference program's by a relative error of at most 0.00053.
Values may be sent and summed in bfloat16 or wider, within the bound.
No kernel may reach another device: no remote copies, remote signals or barrier semaphores. Data moves between devices by JAX's collectives and lax.ppermute only.
A program may use at most 128 MiB of HBM per device.

```python
import math
import jax
import jax.numpy as jnp
from jax import lax

S = 24
H1 = 1600
H2 = 800
H3 = 400
CX = 16
CY = 16
NZ = 128
SUBSTEPS = 2
BLOCK = 128
BWORK = 8
BCAP = 32
RCAP = 4096
CELLS_DEV = 32768
NX = 64
NY = 128
GROUPS_X = 4
GROUPS_Y = 8


def draw_velocity(key, part):
    noise = jnp.clip(jax.random.normal(jax.random.fold_in(key, 21), (3, NX, NY, NZ), jnp.float32), -4.0, 4.0)
    return noise


def draw_react_index(key, part):
    keys = jax.random.split(jax.random.fold_in(key, 11), GROUPS_X * GROUPS_Y)

    def one_list(single):
        return jax.random.permutation(single, CELLS_DEV)[:RCAP]
    lists = jax.vmap(one_list)(keys)
    return lists.reshape(GROUPS_X, GROUPS_Y, RCAP).astype(jnp.int32)


def draw_react_count(key, part):
    most = GROUPS_Y * BWORK
    drops = jax.random.randint(jax.random.fold_in(key, 1), (GROUPS_X,), 0, most // 4 + 1)
    fullest = jax.random.randint(jax.random.fold_in(key, 2), (), 0, GROUPS_X)
    drops = jnp.where(jnp.arange(GROUPS_X) == fullest, 0, drops)
    target = most - drops
    chosen = jax.random.randint(jax.random.fold_in(key, 3), (GROUPS_X,), 0, GROUPS_Y)
    places = jnp.arange(GROUPS_Y)
    is_chosen = places[None, :] == chosen[:, None]
    weights = jax.random.randint(jax.random.fold_in(key, 4), (GROUPS_X, GROUPS_Y), 1, 8)
    weights = jnp.where(is_chosen, 0, weights)
    remain = target - BCAP - (GROUPS_Y - 1)
    shares = remain[:, None] * weights // jnp.sum(weights, axis=1)[:, None]
    leftover = remain - jnp.sum(shares, axis=1)
    ordinal = places[None, :] - (places[None, :] > chosen[:, None]).astype(jnp.int32)
    extra = ((ordinal < leftover[:, None]) & jnp.logical_not(is_chosen)).astype(jnp.int32)
    blocks = jnp.where(is_chosen, BCAP, 1 + shares + extra)
    tails = jax.random.randint(jax.random.fold_in(key, 5), (GROUPS_X, GROUPS_Y), 1, BLOCK + 1)
    counts = jnp.where(is_chosen, BCAP * BLOCK, (blocks - 1) * BLOCK + tails)
    return counts.astype(jnp.int32)


def block_levels(rng, shape, pieces, low, largest):
    def one(axis_at, parts):
        draws = jax.random.uniform(jax.random.fold_in(jax.random.fold_in(rng, 6), axis_at), (parts,), jnp.float32, low / len(pieces), largest / len(pieces))
        return jnp.repeat(jnp.exp(draws), shape[axis_at] // parts).reshape((-1,) + (1,) * (len(shape) - axis_at - 1))

    factor_of = one(*pieces[0])
    for cut in pieces[1:]:
        factor_of = factor_of * one(*cut)
    return factor_of


def gaussian(stream_key, extent, scale, reach, cuts=(), held_as=jnp.bfloat16):
    entries = jax.random.normal(stream_key, extent, jnp.float32) * scale
    if len(cuts) > 0:
        entries = block_levels(stream_key, extent, cuts, -0.22, 0.18) * entries
    return jnp.clip(entries, min=-reach, max=reach).astype(held_as)


def setup_inputs(seed: int = 0) -> dict:
    key_list = jax.random.split(jax.random.key(seed), 12)
    species = gaussian(key_list[0], (S, NX, NY, NZ), 1.0, 6.0, ((1, 4), (2, 8)), jnp.float32)
    diffusivity = jnp.clip(jnp.exp(math.log(2.0) - 1.3862944 * jax.random.uniform(key_list[1], (NX, NY, NZ), jnp.float32) ** block_levels(key_list[1], (NX, NY, NZ), ((0, 4), (1, 8)), -0.2, 0.2)), 0.5, 2.0)
    lewis_number = jnp.clip(jnp.exp(jax.random.uniform(key_list[2], (S,), jnp.float32, math.log(0.5), math.log(2.0))), 0.5, 2.0)
    velocity = draw_velocity(jax.random.fold_in(key_list[11], 71), 0)
    layer_one = gaussian(key_list[4], (H1, S), S ** -0.5, 1.25)
    layer_two = gaussian(key_list[5], (H2, H1), H1 ** -0.5, 0.15625)
    layer_three = gaussian(key_list[6], (H3, H2), H2 ** -0.5, 0.21875)
    layer_four = gaussian(key_list[7], (S, H3), H3 ** -0.5, 0.3125)
    heat_release = gaussian(key_list[8], (S,), 0.5, 3.0, (), jnp.float32)
    react_index = draw_react_index(jax.random.fold_in(key_list[11], 71), 0)
    react_count = draw_react_count(jax.random.fold_in(key_list[11], 71), 0)
    return dict(species=species, diffusivity=diffusivity, lewis_number=lewis_number, velocity=velocity, layer_one=layer_one, layer_two=layer_two, layer_three=layer_three, layer_four=layer_four, heat_release=heat_release, react_index=react_index, react_count=react_count)


diffuse_step = 0.03
react_step = 0.5


def diffuse_whole(values, coeffs):
    terms = []
    for axis in range(3):
        after = jnp.roll(values, -1, axis)
        before = jnp.roll(values, 1, axis)
        coef_after = jnp.roll(coeffs, -1, axis)
        coef_before = jnp.roll(coeffs, 1, axis)
        upward = 0.5 * (coeffs + coef_after) * (after - values)
        downward = 0.5 * (coef_before + coeffs) * (values - before)
        terms.append(upward - downward)
    return values + diffuse_step * ((terms[0] + terms[1]) + terms[2])


def network_rows(rows, first, second, third, fourth):
    hidden = jax.nn.silu(jnp.dot(rows, first.T, preferred_element_type=jnp.float32)).astype(jnp.bfloat16)
    hidden = jax.nn.silu(jnp.dot(hidden, second.T, preferred_element_type=jnp.float32)).astype(jnp.bfloat16)
    hidden = jax.nn.silu(jnp.dot(hidden, third.T, preferred_element_type=jnp.float32)).astype(jnp.bfloat16)
    return jnp.dot(hidden, fourth.T, preferred_element_type=jnp.float32).astype(jnp.bfloat16)


def inverse_symbol(wave_x, wave_y, wave_z, size_x, size_y, size_z):
    along_x = 2.0 * jnp.cos(wave_x.astype(jnp.float32) * (2.0 * jnp.pi / size_x)) - 2.0
    along_y = 2.0 * jnp.cos(wave_y.astype(jnp.float32) * (2.0 * jnp.pi / size_y)) - 2.0
    along_z = 2.0 * jnp.cos(wave_z.astype(jnp.float32) * (2.0 * jnp.pi / size_z)) - 2.0
    symbol = along_x[:, None, None] + along_y[None, :, None] + along_z[None, None, :]
    anchor = (wave_x[:, None, None] == 0) & (wave_y[None, :, None] == 0) & (wave_z[None, None, :] == 0)
    return jnp.where(anchor, 0.0, 1.0 / jnp.where(anchor, 1.0, symbol))


def reference(species, diffusivity, lewis_number, velocity, layer_one, layer_two, layer_three, layer_four, heat_release, react_index, react_count):
    def one_species(packed):
        values, lewis = packed
        coeffs = diffusivity / lewis
        for substep in range(SUBSTEPS):
            values = diffuse_whole(values, coeffs)
        return values

    diffused = lax.map(one_species, (species, lewis_number))
    flat_fields = diffused.reshape(S, NX * NY * NZ)

    live_blocks = ((react_count + BLOCK - 1) // BLOCK).astype(jnp.int32)
    starts = (jnp.cumsum(live_blocks, axis=1) - live_blocks).astype(jnp.int32)
    slot_ids = jnp.arange(GROUPS_Y * BWORK, dtype=jnp.int32)
    row_ids = jnp.arange(BLOCK, dtype=jnp.int32)

    def group_rows(packed):
        starts_row, live_row, counts_row, index_rows, column = packed
        owner = jnp.sum((starts_row[None, :] <= slot_ids[:, None]).astype(jnp.int32), axis=1) - 1
        block = slot_ids - starts_row[owner]
        valid = block < live_row[owner]
        block = jnp.where(valid, block, 0).astype(jnp.int32)
        position = (block[:, None] * BLOCK + row_ids[None, :]).astype(jnp.int32)
        local = index_rows[owner[:, None], position]
        living = valid[:, None] & (position < counts_row[owner][:, None])
        cell_x = column * CX + local // (CY * NZ)
        cell_y = owner[:, None] * CY + (local // NZ) % CY
        cell_z = local % NZ
        global_ids = ((cell_x * NY + cell_y) * NZ + cell_z).astype(jnp.int32).reshape(-1)
        rows = flat_fields[:, global_ids].T.astype(jnp.bfloat16)
        rate_rows = network_rows(rows, layer_one, layer_two, layer_three, layer_four)
        return global_ids, living.reshape(-1), rate_rows

    columns = jnp.arange(GROUPS_X, dtype=jnp.int32)
    global_ids, living, rate_rows = lax.map(group_rows, (starts, live_blocks, react_count, react_index, columns))
    global_ids = global_ids.reshape(-1)
    living = living.reshape(-1)
    rate_rows = rate_rows.reshape(-1, S).astype(jnp.float32)
    update = jnp.where(living[:, None], react_step * rate_rows, 0.0)
    species_out = flat_fields.at[:, global_ids].add(update.T).reshape(S, NX, NY, NZ)
    heat_rows = jnp.where(living, jnp.dot(rate_rows, heat_release, precision=lax.Precision.HIGHEST), 0.0)
    heat = jnp.zeros((NX * NY * NZ,), jnp.float32).at[global_ids].add(heat_rows).reshape(NX, NY, NZ)

    divergence = (jnp.roll(velocity[0], -1, 0) - velocity[0]) + (jnp.roll(velocity[1], -1, 1) - velocity[1]) + (jnp.roll(velocity[2], -1, 2) - velocity[2])
    source = divergence - heat
    symbol = inverse_symbol(jnp.arange(NX, dtype=jnp.int32), jnp.arange(NY, dtype=jnp.int32), jnp.arange(NZ, dtype=jnp.int32), NX, NY, NZ)
    pressure = jnp.real(jnp.fft.ifftn(jnp.fft.fftn(source) * symbol)).astype(species.dtype)
    gradient = jnp.stack([pressure - jnp.roll(pressure, 1, 0), pressure - jnp.roll(pressure, 1, 1), pressure - jnp.roll(pressure, 1, 2)])
    velocity_out = velocity - gradient
    return species_out, velocity_out
```

```python
import functools

import jax
import jax.numpy as jnp
import numpy as np
from jax import lax
from jax.experimental import pallas as pl
from jax.experimental.pallas import tpu as pltpu
from jax.sharding import PartitionSpec as P

SUBSTEPS = 2
LANES = 128
diffuse_step = 0.03
react_step = 0.5

f32 = jnp.float32
bf16 = jnp.bfloat16
HIGHEST = lax.Precision.HIGHEST
VMEM_LIMIT = 48 * 2**20
PADW = 20
PADK = 24
TILE = 512


def dot(a, b, precision=None):
    return jnp.dot(a, b, preferred_element_type=f32, precision=precision)


def dot_nt(a, b):
    return lax.dot_general(a, b, (((1,), (1,)), ((), ())), preferred_element_type=f32)


def spec_vmem():
    return pl.BlockSpec(memory_space=pltpu.VMEM)


def spec_smem():
    return pl.BlockSpec(memory_space=pltpu.SMEM)


def silu(value):
    half = 0.5 * value
    return half * jnp.tanh(half) + half


def pack_kernel(sp_ref, kappa_ref, vel_ref, grid_ref, ylo_ref, yhi_ref, xlo_ref, xhi_ref, *, wx, wy, kinds):
    rows = wx * wy

    @pl.loop(0, wx)
    def _(x):
        for y in range(wy):
            line = sp_ref[pl.ds(x * wy + y, kinds, stride=rows), :]
            grid_ref[(x + 2) * PADW + y + 2] = line

    def split(value):
        high = value.astype(bf16)
        low = (value - high.astype(f32)).astype(bf16)
        return high, low

    def cell(x, y):
        return grid_ref[(x + 2) * PADW + y + 2]

    pair = 2 * kinds
    for ref, first in ((ylo_ref, 0), (yhi_ref, wy - 2)):
        for x in range(wx):
            ref[pl.ds(x * pair, pair), :] = jnp.concatenate(
                [cell(x, first), cell(x, first + 1)], axis=0
            ).astype(bf16)
        base = wx * pair
        for k in range(2):
            high, low = split(kappa_ref[pl.ds(first + k, wx, stride=wy), :])
            ref[pl.ds(base + k * wx, wx), :] = high
            ref[pl.ds(base + (2 + k) * wx, wx), :] = low
        high, low = split(vel_ref[pl.ds(rows + first, wx, stride=wy), :])
        ref[pl.ds(base + 4 * wx, wx), :] = high
        ref[pl.ds(base + 5 * wx, wx), :] = low
    for ref, planes in ((xlo_ref, (0, 1)), (xhi_ref, (wx - 1, wx - 2))):
        for k, x in enumerate(planes):
            for y in range(0, wy, 2):
                ref[pl.ds(k * wy * kinds + y * kinds, pair), :] = jnp.concatenate(
                    [cell(x, y), cell(x, y + 1)], axis=0
                ).astype(bf16)
        base = 2 * wy * kinds
        for k, x in enumerate(planes):
            high, low = split(kappa_ref[pl.ds(x * wy, wy), :])
            ref[pl.ds(base + k * wy, wy), :] = high
            ref[pl.ds(base + (2 + k) * wy, wy), :] = low
        high, low = split(vel_ref[pl.ds(planes[0] * wy, wy), :])
        ref[pl.ds(base + 4 * wy, wy), :] = high
        ref[pl.ds(base + 5 * wy, wy), :] = low


def list_kernel(count_ref, index_ref, before_ref, beforet_ref, upper_ref, table_ref, place_ref, offset_ref, onerow, onecol, *, rows):
    count = count_ref[0]
    capacity = index_ref.shape[1]
    step = 512
    parts = capacity // step

    def parts_of(j):
        number = index_ref[:, pl.ds(j * step, step)]
        valid = (lax.broadcasted_iota(jnp.int32, (1, step), 1) + j * step) < count
        row = jnp.where(valid, number // LANES, -1)
        return row, number % LANES, valid

    mask = jnp.zeros((rows, LANES), f32)
    for j in range(parts):
        row, col, valid = parts_of(j)
        hit = lax.broadcasted_iota(jnp.int32, (rows, step), 0) == row
        onerow[:, j * step : (j + 1) * step] = hit.astype(f32).astype(bf16)
        hit = lax.broadcasted_iota(jnp.int32, (LANES, step), 0) == col
        onecol[:, j * step : (j + 1) * step] = hit.astype(f32).astype(bf16)
    mask = dot_nt(onerow[...], onecol[...])
    maskb = mask.astype(bf16)
    rank = dot(maskb, upper_ref[...])
    total = dot(maskb, jnp.ones((LANES, LANES), bf16))
    offset = dot(before_ref[...], total.astype(bf16))
    total_row = dot_nt(jnp.ones((8, LANES), bf16), maskb)
    offset_ref[...] = dot(total_row.astype(bf16), beforet_ref[...]).astype(jnp.int32)
    place = (offset + rank).astype(jnp.int32)
    place_hi = (place // LANES).astype(f32)
    place_lo = (place % LANES).astype(f32)
    place_ref[...] = jnp.where(mask > 0.5, place % LANES, place % LANES - LANES)
    both = jnp.concatenate([place_hi.T, place_lo.T], axis=0).astype(bf16)
    table = jnp.zeros(table_ref.shape, f32)
    for j in range(parts):
        row, col, valid = parts_of(j)
        found = dot(both, onerow[:, j * step : (j + 1) * step])
        colf = onecol[:, j * step : (j + 1) * step].astype(f32)
        hi = jnp.sum(found[:LANES] * colf, axis=0, keepdims=True)
        lo = jnp.sum(found[LANES:] * colf, axis=0, keepdims=True)
        hi = jnp.where(valid, hi, -1.0).astype(jnp.int32)
        lo = lo.astype(jnp.int32)
        put_hi = jnp.where(
            lax.broadcasted_iota(jnp.int32, (table_ref.shape[0], step), 0) == hi,
            col.astype(f32),
            0.0,
        ).astype(bf16)
        put_lo = (
            (lax.broadcasted_iota(jnp.int32, (LANES, step), 0) == lo).astype(f32).astype(bf16)
        )
        table = table + dot_nt(put_hi, put_lo)
    table_ref[...] = table.astype(jnp.int32)


def make_weights(kp, we, wn, wu, wd, ws, wx):
    scale = 0.5 * diffuse_step

    def line(px):
        base = px * PADK
        here = kp[pl.ds(base, PADK), :]
        up = jnp.roll(here, -1, 1)
        wu_v = scale * (here + up)
        we_v = scale * (here + kp[pl.ds(base + PADK, PADK), :])
        wn_v = scale * (here + kp[pl.ds(base + 1, PADK), :])
        ww_v = scale * (here + kp[pl.ds(base - PADK, PADK), :])
        wsouth = scale * (here + kp[pl.ds(base - 1, PADK), :])
        wd_v = jnp.roll(wu_v, 1, 1)
        we[pl.ds(base, PADK), :] = we_v
        wn[pl.ds(base, PADK), :] = wn_v
        wu[pl.ds(base, PADK), :] = wu_v
        wd[pl.ds(base, PADK), :] = wd_v
        ws[pl.ds(base, PADK), :] = ((we_v + ww_v) + (wn_v + wsouth)) + (wu_v + wd_v)

    for px in range(1, wx + 3):
        line(px)
    base = 0
    here = kp[pl.ds(base, PADK), :]
    we[pl.ds(base, PADK), :] = scale * (here + kp[pl.ds(base + PADK, PADK), :])


def cell_update(src, px, py, weights, lewis):
    we, wn, wu, wd, ws = weights
    row = px * PADW + py
    kr = px * PADK + py

    def w(ref, r):
        return ref[pl.ds(r, 1), :]

    here = src[row]
    total = w(we, kr) * src[row + PADW] + w(we, kr - PADK) * src[row - PADW]
    total = total + (w(wn, kr) * src[row + 1] + w(wn, kr - 1) * src[row - 1])
    total = total + (w(wu, kr) * jnp.roll(here, -1, 1) + w(wd, kr) * jnp.roll(here, 1, 1))
    total = total - w(ws, kr) * here
    return here + lewis * total


def transport_kernel(
    count_ref,
    offset_ref,
    order_ref,
    heat_ref,
    grid_ref,
    kappa_ref,
    lewis_ref,
    vel_ref,
    yprev_ref,
    ynext_ref,
    xprev_ref,
    xnext_ref,
    table_ref,
    place_ref,
    w1_ref,
    w2_ref,
    w3_ref,
    w4_ref,
    zmat_ref,
    out_ref,
    spec_ref,
    p0,
    p1,
    p2,
    kp,
    we,
    wn,
    wu,
    wd,
    ws,
    compact,
    rates,
    heat_rows,
    *,
    wx,
    wy,
    kinds,
):
    rows = wx * wy
    pair = 2 * kinds
    weights = (we, wn, wu, wd, ws)
    lewis = jnp.broadcast_to(1.0 / lewis_ref[...], (kinds, LANES))
    p0[...] = grid_ref[...]
    for x in range(wx):
        kp[pl.ds((x + 2) * PADK + 2, wy), :] = kappa_ref[pl.ds(x * wy, wy), :]
    ybase = wx * pair
    for ref, py in ((yprev_ref, 0), (ynext_ref, wy + 2)):
        for x in range(wx):
            both = ref[pl.ds(x * pair, pair), :].astype(f32)
            p0[(x + 2) * PADW + py] = both[:kinds]
            p0[(x + 2) * PADW + py + 1] = both[kinds:]
        for k in range(2):
            value = ref[pl.ds(ybase + k * wx, wx), :].astype(f32) + ref[
                pl.ds(ybase + (2 + k) * wx, wx), :
            ].astype(f32)
            kp[pl.ds(2 * PADK + py + k, wx, stride=PADK), :] = value
    xbase = 2 * wy * kinds
    cbase = xbase + 6 * wy
    for ref, near, far, edge in ((xprev_ref, 1, 0, wx - 1), (xnext_ref, wx + 2, wx + 3, 0)):
        for k, px in ((0, near), (1, far)):
            for y in range(0, wy, 2):
                both = ref[pl.ds(k * wy * kinds + y * kinds, pair), :].astype(f32)
                p0[px * PADW + y + 2] = both[:kinds]
                p0[px * PADW + y + 3] = both[kinds:]
            value = ref[pl.ds(xbase + k * wy, wy), :].astype(f32) + ref[
                pl.ds(xbase + (2 + k) * wy, wy), :
            ].astype(f32)
            kp[pl.ds(px * PADK + 2, wy), :] = value
        piece = pair + 2 * wx
        for k, py in ((0, 1), (1, wy + 2)):
            start = cbase + k * piece
            both = ref[pl.ds(start, pair), :].astype(f32)
            p0[near * PADW + py] = both[kinds:] if k == 0 else both[:kinds]
            value = ref[pl.ds(start + pair, wx), :].astype(f32) + ref[
                pl.ds(start + pair + wx, wx), :
            ].astype(f32)
            kp[pl.ds(near * PADK + py, 1), :] = value[edge : edge + 1]
    make_weights(kp, we, wn, wu, wd, ws, wx)

    for px in (1, wx + 2):
        for py in range(2, wy + 2):
            p1[px * PADW + py] = cell_update(p0, px, py, weights, lewis)

    @pl.loop(2, wx + 2)
    def _(px):
        for py in range(1, wy + 3):
            p1[px * PADW + py] = cell_update(p0, px, py, weights, lewis)

    @pl.loop(2, wx + 2)
    def _(px):
        for py in range(2, wy + 2):
            p2[(px - 2) * wy + py - 2] = cell_update(p1, px, py, weights, lewis)

    lane = lax.broadcasted_iota(jnp.int32, (1, LANES), 1)

    @pl.loop(0, rows, unroll=8)
    def _(q):
        r = order_ref[q]
        offset = offset_ref[0, r]
        hi = offset // LANES
        lo = offset % LANES
        later = lane >= lo
        pick = jnp.where(later, table_ref[pl.ds(hi, 1), :], table_ref[pl.ds(hi + 1, 1), :])
        got = jnp.take_along_axis(
            p2[r], jnp.broadcast_to(pick, (kinds, LANES)), axis=1, mode="promise_in_bounds"
        )
        pltpu.store(compact.at[hi], got, mask=jnp.broadcast_to(later, (kinds, LANES)))
        compact[hi + 1] = got

    count = count_ref[0]

    @pl.loop(0, (count + TILE - 1) // TILE)
    def _(t):
        blocks = TILE // LANES
        cells = jnp.concatenate([compact[t * blocks + k] for k in range(blocks)], axis=1)
        hidden = silu(dot(w1_ref[...], cells.astype(bf16))).astype(bf16)
        hidden = silu(dot(w2_ref[...], hidden)).astype(bf16)
        hidden = silu(dot(w3_ref[...], hidden)).astype(bf16)
        result = dot(w4_ref[...], hidden).astype(bf16).astype(f32)
        for k in range(blocks):
            rates[t * blocks + k] = result[:, k * LANES : (k + 1) * LANES]

    release = jnp.broadcast_to(heat_ref[...], (kinds, LANES))

    @pl.loop(0, rows, unroll=8)
    def _(r):
        offset = offset_ref[0, r]
        hi = offset // LANES
        lo = offset % LANES
        merged = jnp.where(
            jnp.broadcast_to(lane >= lo, (kinds, LANES)), rates[hi], rates[hi + 1]
        )
        place = place_ref[pl.ds(r, 1), :]
        live = jnp.broadcast_to(place >= 0, (kinds, LANES))
        pick = jnp.broadcast_to(place & (LANES - 1), (kinds, LANES))
        got = jnp.take_along_axis(merged, pick, axis=1, mode="promise_in_bounds")
        got = jnp.where(live, got, 0.0)
        spec_ref[pl.ds(r, kinds, stride=rows), :] = p2[r] + react_step * got
        heat_rows[pl.ds(r, 1), :] = jnp.sum(release * got, axis=0, keepdims=True)

    ux = vel_ref[pl.ds(0, rows), :]
    nextx = xnext_ref[pl.ds(xbase + 4 * wy, wy), :].astype(f32) + xnext_ref[
        pl.ds(xbase + 5 * wy, wy), :
    ].astype(f32)
    east = jnp.concatenate([ux[wy:], nextx], axis=0)
    nexty = ynext_ref[pl.ds(ybase + 4 * wx, wx), :].astype(f32) + ynext_ref[
        pl.ds(ybase + 5 * wx, wx), :
    ].astype(f32)
    uy = vel_ref[pl.ds(rows, rows), :]
    north = vel_ref[pl.ds(rows + 1, rows), :]
    last = lax.broadcasted_iota(jnp.int32, (wy, LANES), 0) == wy - 1
    pieces = []
    for x in range(wx):
        pieces.append(
            jnp.where(
                last,
                jnp.broadcast_to(nexty[x : x + 1], (wy, LANES)),
                north[x * wy : (x + 1) * wy],
            )
        )
    north = jnp.concatenate(pieces, axis=0)
    uz = vel_ref[pl.ds(2 * rows, rows), :]
    source = (east - ux) + (north - uy) + (jnp.roll(uz, -1, 1) - uz) - heat_rows[...]
    turned = jnp.concatenate(
        [source[h * LANES : (h + 1) * LANES].T for h in range(rows // LANES)], axis=0
    )
    out_ref[...] = dot(zmat_ref[...], turned, HIGHEST)


def solve_kernel(
    in_ref, lam_ref, lamy_ref, qy_ref, qyt_ref, bx_ref, bxt_ref, pick_ref, kind_ref, out_ref, lines, tiles, *, na, nb, wide, keep
):
    groups = LANES // wide
    spans = nb // groups
    lane = lax.broadcasted_iota(jnp.int32, (1, LANES), 1) // wide
    for a in range(na):
        for span in range(spans):
            blocks = [
                in_ref[pl.ds((a * nb + span * groups + g) * keep, keep), :] for g in range(groups)
            ]
            for g in range(groups):
                line = blocks[g]
                for b in range(groups):
                    if b != g:
                        moved = pltpu.roll(blocks[b], ((b - g) * wide) % LANES, 1)
                        line = jnp.where(lane == b, moved, line)
                lines[pl.ds((g * na + a) * keep, keep), span * LANES : (span + 1) * LANES] = line
    wave = dot(bx_ref[...], dot(lines[...], qyt_ref[...], HIGHEST), HIGHEST)
    lam = lam_ref[...] + lamy_ref[...]
    anchor = lam == 0.0
    wave = jnp.where(anchor, 0.0, wave / jnp.where(anchor, 1.0, lam))
    lines[...] = dot(dot(bxt_ref[...], wave, HIGHEST), qy_ref[...], HIGHEST)
    for a in range(na):
        for span in range(spans):
            blocks = [
                lines[pl.ds((g * na + a) * keep, keep), span * LANES : (span + 1) * LANES]
                for g in range(groups)
            ]
            for b in range(groups):
                tile = blocks[b]
                for g in range(groups):
                    if b != g:
                        moved = pltpu.roll(blocks[g], ((g - b) * wide) % LANES, 1)
                        tile = jnp.where(lane == g, moved, tile)
                where = a * nb + span * groups + b
                tiles[pl.ds(where * keep, keep), :] = tile
                out_ref[pl.ds(where * (keep + 1), keep), :] = tile
    south_pick = pick_ref[pl.ds(0, keep), :]
    west_pick = pick_ref[pl.ds(keep, keep), :]
    kind = kind_ref[...]
    for a in range(na):
        for b in range(nb):
            south = tiles[pl.ds((a * nb + (b - 1) % nb) * keep, keep), :]
            west = tiles[pl.ds(((a - 1) % na * nb + b) * keep, keep), :]
            south = jnp.take_along_axis(south, south_pick, axis=1, mode="promise_in_bounds")
            west = jnp.take_along_axis(west, west_pick, axis=1, mode="promise_in_bounds")
            both = jnp.where(kind == 1, south, jnp.where(kind == 2, west, 0.0))
            out_ref[pl.ds((a * nb + b) * (keep + 1) + keep, 1), :] = jnp.sum(
                both, axis=0, keepdims=True
            )


def slope_kernel(in_ref, inv_ref, vel_ref, out_ref, padded, extra, field, *, wx, wy, modes):
    rows = wx * wy
    halves = rows // LANES
    total = in_ref.shape[0]
    full = padded.shape[0]
    padded[pl.ds(0, total), :] = in_ref[...]
    if full > total:
        padded[pl.ds(total, full - total), :] = jnp.zeros((full - total, LANES), f32)
    turned = jnp.concatenate(
        [padded[pl.ds(k * LANES, LANES), :].T for k in range(full // LANES)], axis=1
    )
    wave = dot(turned, inv_ref[...], HIGHEST)
    for h in range(halves):
        field[pl.ds(wy + h * LANES, LANES), :] = wave[:, h * LANES : (h + 1) * LANES]
    for m in range(modes):
        extra[m] = wave[:, (halves + m) * LANES : (halves + m + 1) * LANES]
    south = []
    west = []
    lines = LANES // wy
    for h in range(halves):
        south.append(sum(extra[m, pl.ds(h * modes + m, lines, stride=wy), :] for m in range(modes)))
    for g in range(2):
        west.append(sum(extra[m, pl.ds((m * 2 + g) * wy + wy // 2, wy // 2), :] for m in range(modes)))
    field[pl.ds(0, wy), :] = jnp.concatenate(west, axis=0)
    here = field[pl.ds(wy, rows), :]
    out_ref[pl.ds(0, rows), :] = vel_ref[pl.ds(0, rows), :] - (here - field[pl.ds(0, rows), :])
    first = lax.broadcasted_iota(jnp.int32, (wy, LANES), 0) == 0
    for x in range(wx):
        behind = field[pl.ds(wy - 1 + x * wy, wy), :]
        edge = south[x // lines][x % lines : x % lines + 1]
        behind = jnp.where(first, jnp.broadcast_to(edge, (wy, LANES)), behind)
        at = pl.ds(rows + x * wy, wy)
        out_ref[at, :] = vel_ref[at, :] - (here[x * wy : (x + 1) * wy] - behind)
    at = pl.ds(2 * rows, rows)
    out_ref[at, :] = vel_ref[at, :] - (here - jnp.roll(here, 1, 1))


def real_basis(n):
    at = np.arange(n)
    basis = np.zeros((n, n))
    waves = np.zeros(n, dtype=np.int64)
    basis[0] = 1.0 / np.sqrt(n)
    for k in range(1, (n + 1) // 2):
        angle = 2.0 * np.pi * ((k * at) % n) / n
        basis[2 * k - 1] = np.sqrt(2.0 / n) * np.cos(angle)
        basis[2 * k] = np.sqrt(2.0 / n) * np.sin(angle)
        waves[2 * k - 1] = k
        waves[2 * k] = k
    if n % 2 == 0:
        basis[n - 1] = np.where(at % 2 == 0, 1.0, -1.0) / np.sqrt(n)
        waves[n - 1] = n // 2
    return basis, -4.0 * np.sin(np.pi * waves / n) ** 2


@functools.lru_cache(maxsize=None)
def plan(wx, wy, depth, na, nb):
    rows = wx * wy
    halves = rows // LANES
    devices = na * nb
    modes = depth // devices
    keep = halves * modes
    lines = LANES // wy
    zb, lamz = real_basis(depth)
    qx, lamx = real_basis(wx * na)
    qy, lamy = real_basis(wy * nb)
    zmat = np.zeros((devices, halves, modes, halves, depth))
    for h in range(halves):
        zmat[:, h, :, h, :] = zb.reshape(devices, modes, depth)
    zmat = zmat.reshape(devices * keep, halves * depth)
    inv = np.zeros((devices, keep + 1, halves + modes, depth))
    for h in range(halves):
        for m in range(modes):
            inv[:, h * modes + m, h, :] = zb.reshape(devices, modes, depth)[:, m]
    for m in range(modes):
        inv[:, keep, halves + m, :] = zb.reshape(devices, modes, depth)[:, m]
    inv = inv.reshape(devices * (keep + 1), (halves + modes) * depth)
    full = -(-inv.shape[0] // LANES) * LANES
    inv = np.pad(inv, ((0, full - inv.shape[0]), (0, 0)))
    bx = np.zeros((wx * na, modes, lines, na, halves, modes))
    for g in range(lines):
        for a in range(na):
            for h in range(halves):
                for m in range(modes):
                    bx[:, m, g, a, h, m] = qx[:, a * wx + h * lines + g]
    bx = bx.reshape(wx * na * modes, lines * na * keep)
    pick = np.zeros((2, keep, LANES), np.int32)
    kind = np.zeros((keep, LANES), np.int32)
    for k in range(keep):
        for g in range(lines):
            pick[0, k, g * wy + k] = g * wy + wy - 1
            kind[k, g * wy + k] = 1
    for m in range(modes):
        for y in range(wy):
            to = (m * 2 + y // (wy // 2)) * wy + wy // 2 + y % (wy // 2)
            pick[1, (halves - 1) * modes + m, to] = LANES - wy + y
            kind[(halves - 1) * modes + m, to] = 2
    inner = [
        x * wy + y for x in range(wx) for y in range(wy) if 2 <= x < wx - 2 and 2 <= y < wy - 2
    ]
    outer = [r for r in range(rows) if r not in set(inner)]
    order = np.array(inner + outer)
    turn = np.empty(rows, np.int64)
    turn[order] = np.arange(rows)
    before = turn[None, :] < turn[:, None]
    upper = np.arange(LANES)[:, None] < np.arange(LANES)[None, :]
    as32 = lambda v: np.asarray(v, np.float32)
    as16 = lambda v: np.asarray(v, np.float32).astype(jnp.bfloat16)
    return dict(
        zmat=as32(zmat),
        inv=as32(inv),
        bx=as32(bx),
        bxt=as32(bx.T),
        qy=as32(qy),
        qyt=as32(qy.T),
        lamx=as32(np.repeat(lamx, modes)[:, None]),
        lamy=as32(lamy[None, :]),
        lamz=as32(lamz),
        pick=pick.reshape(2 * keep, LANES),
        kind=kind,
        order=order.astype(np.int32),
        before=as16(before),
        beforet=as16(before.T),
        upper=as16(upper),
        inner=len(inner),
    )


def shift(value, axis, by):
    peers = lax.axis_size(axis)
    return lax.ppermute(value, axis, [(i, (i + by) % peers) for i in range(peers)])


def params():
    return pltpu.CompilerParams(vmem_limit_bytes=VMEM_LIMIT)


def per_device(
    species,
    diffusivity,
    lewis_number,
    velocity,
    layer_one,
    layer_two,
    layer_three,
    layer_four,
    heat_release,
    react_index,
    react_count,
):
    kinds, wx, wy, depth = species.shape
    na = lax.axis_size("gx")
    nb = lax.axis_size("gy")
    devices = na * nb
    rows = wx * wy
    halves = rows // LANES
    modes = depth // devices
    keep = halves * modes
    tab = plan(wx, wy, depth, na, nb)
    sp = species.reshape(kinds * rows, depth)
    kappa = diffusivity.reshape(rows, depth)
    vel = velocity.reshape(3 * rows, depth)
    count = react_count.reshape(1)
    capacity = react_index.size
    slots = capacity // LANES
    sds = jax.ShapeDtypeStruct
    own = 2 * wy * kinds + 6 * wy

    grid, ylo, yhi, xlo, xhi = pl.pallas_call(
        functools.partial(pack_kernel, wx=wx, wy=wy, kinds=kinds),
        out_shape=[sds((PADW * PADW, kinds, depth), f32)] + [sds((own, depth), bf16)] * 4,
        in_specs=[spec_vmem()] * 3,
        out_specs=[spec_vmem()] * 5,
        compiler_params=params(),
        name="pack",
    )(sp, kappa, vel)

    yprev = shift(yhi, "gy", 1)
    ynext = shift(ylo, "gy", -1)

    pair = 2 * kinds
    ybase = wx * pair

    def corner(ref, x, k):
        return [
            ref[x * pair : (x + 1) * pair],
            ref[ybase + k * wx : ybase + (k + 1) * wx],
            ref[ybase + (2 + k) * wx : ybase + (3 + k) * wx],
        ]

    xlo = jnp.concatenate([xlo] + corner(yprev, 0, 1) + corner(ynext, 0, 0), axis=0)
    xhi = jnp.concatenate([xhi] + corner(yprev, wx - 1, 1) + corner(ynext, wx - 1, 0), axis=0)
    xprev = shift(xhi, "gx", 1)
    xnext = shift(xlo, "gx", -1)

    table, place, offset = pl.pallas_call(
        functools.partial(list_kernel, rows=rows),
        out_shape=[
            sds((slots + 8, LANES), jnp.int32),
            sds((rows, LANES), jnp.int32),
            sds((8, rows), jnp.int32),
        ],
        in_specs=[spec_smem()] + [spec_vmem()] * 4,
        out_specs=[spec_vmem()] * 3,
        scratch_shapes=[
            pltpu.VMEM((rows, capacity), bf16),
            pltpu.VMEM((LANES, capacity), bf16),
        ],
        compiler_params=params(),
        name="lists",
    )(
        count,
        react_index.reshape(1, capacity),
        tab["before"],
        tab["beforet"],
        tab["upper"],
    )

    weight_rows = pltpu.VMEM((PADW * PADK + 8, depth), f32)
    wave, species_out = pl.pallas_call(
        functools.partial(transport_kernel, wx=wx, wy=wy, kinds=kinds),
        out_shape=[sds((devices * keep, LANES), f32), sds((kinds * rows, depth), f32)],
        in_specs=[spec_smem()] * 3 + [spec_vmem()] * 16,
        out_specs=[spec_vmem()] * 2,
        scratch_shapes=[
            pltpu.VMEM((PADW * PADW, kinds, depth), f32),
            pltpu.VMEM((PADW * PADW, kinds, depth), f32),
            pltpu.VMEM((rows, kinds, depth), f32),
        ]
        + [weight_rows] * 6
        + [
            pltpu.VMEM((slots + 8, kinds, LANES), f32),
            pltpu.VMEM((slots + 8, kinds, LANES), f32),
            pltpu.VMEM((rows, depth), f32),
        ],
        compiler_params=params(),
        name="transport",
    )(
        count,
        offset,
        tab["order"],
        heat_release.reshape(kinds, 1),
        grid,
        kappa,
        lewis_number.reshape(kinds, 1),
        vel,
        yprev,
        ynext,
        xprev,
        xnext,
        table,
        place,
        layer_one,
        layer_two,
        layer_three,
        layer_four,
        tab["zmat"],
    )

    wave = lax.all_to_all(wave, ("gx", "gy"), 0, 0, tiled=True)

    me = lax.axis_index("gx") * nb + lax.axis_index("gy")
    lam_here = lax.dynamic_slice(jnp.asarray(tab["lamz"]), (me * modes,), (modes,))
    lam = tab["lamx"] + jnp.tile(lam_here, wx * na)[:, None]
    plane_rows = wx * na * modes
    back = pl.pallas_call(
        functools.partial(solve_kernel, na=na, nb=nb, wide=wy, keep=keep),
        out_shape=sds((devices * (keep + 1), LANES), f32),
        in_specs=[spec_vmem()] * 9,
        out_specs=spec_vmem(),
        scratch_shapes=[
            pltpu.VMEM((plane_rows, wy * nb), f32),
            pltpu.VMEM((devices * keep, LANES), f32),
        ],
        compiler_params=params(),
        name="solve",
    )(
        wave,
        lam,
        tab["lamy"],
        tab["qy"],
        tab["qyt"],
        tab["bx"],
        tab["bxt"],
        tab["pick"],
        tab["kind"],
    )

    back = lax.all_to_all(back, ("gx", "gy"), 0, 0, tiled=True)

    velocity_out = pl.pallas_call(
        functools.partial(slope_kernel, wx=wx, wy=wy, modes=modes),
        out_shape=sds((3 * rows, depth), f32),
        in_specs=[spec_vmem()] * 3,
        out_specs=spec_vmem(),
        scratch_shapes=[
            pltpu.VMEM((tab["inv"].shape[0], LANES), f32),
            pltpu.VMEM((modes, LANES, depth), f32),
            pltpu.VMEM((rows + wy, depth), f32),
        ],
        compiler_params=params(),
        name="slope",
    )(back, tab["inv"], vel)
    return (species_out.reshape(species.shape), velocity_out.reshape(velocity.shape))


def solution(mesh):
    return jax.shard_map(
        per_device,
        mesh=mesh,
        in_specs=(
            P(None, "gx", "gy", None),
            P("gx", "gy", None),
            P(),
            P(None, "gx", "gy", None),
            P(),
            P(),
            P(),
            P(),
            P(),
            P("gx", "gy", None),
            P("gx", "gy"),
        ),
        out_specs=(P(None, "gx", "gy", None), P(None, "gx", "gy", None)),
        check_vma=False,
    )
```

```python
import functools

import jax
import jax.numpy as jnp
import numpy as np
from jax import lax
from jax.experimental import pallas as pl
from jax.experimental.pallas import tpu as pltpu
from jax.sharding import PartitionSpec as P

SUBSTEPS = 2
LANES = 128
diffuse_step = 0.03
react_step = 0.5

f32 = jnp.float32
bf16 = jnp.bfloat16
HIGHEST = lax.Precision.HIGHEST
GAP = 8
BATCH = 8
PADW = 20
PADK = 24
TILE = 512


def dot(a, b, precision=None):
    return jnp.dot(a, b, preferred_element_type=f32, precision=precision)


def dot_nt(a, b):
    return lax.dot_general(a, b, (((1,), (1,)), ((), ())), preferred_element_type=f32)


def spec_vmem():
    return pl.BlockSpec(memory_space=pltpu.VMEM)


def spec_smem():
    return pl.BlockSpec(memory_space=pltpu.SMEM)


def silu(value):
    half = 0.5 * value
    return half * jnp.tanh(half) + half


def spec_any():
    return pl.BlockSpec(memory_space=pl.ANY)


def spec_hbm():
    return pl.BlockSpec(memory_space=pltpu.HBM)


def start_all(pairs, sems):
    copies = [pltpu.make_async_copy(a, b, sems.at[k]) for k, (a, b) in enumerate(pairs)]
    for copy in copies:
        copy.start()
    return copies


def wait_all(copies):
    for copy in copies:
        copy.wait()


def split(value):
    high = value.astype(bf16)
    low = (value - high.astype(f32)).astype(bf16)
    return high, low


def load_species(sp_hbm, sp_pad, rows):
    return [(sp_hbm, sp_pad.at[:, pl.ds(0, rows)])]


def as_lines(ref):
    return ref.reshape(ref.shape[0] * ref.shape[1], *ref.shape[2:])


def y_message_kernel(
    sp_hbm, kappa_hbm, vel_hbm, ylo_ref, yhi_ref, sp_pad, kappa_ref, vel_ref, sems, *, wx, wy, kinds
):
    rows = wx * wy
    pair = 2 * kinds
    step = rows + GAP
    pairs = load_species(sp_hbm, sp_pad, rows)
    sp_ref = as_lines(sp_pad)
    wait_all(start_all([(kappa_hbm, kappa_ref), (vel_hbm, vel_ref)] + pairs, sems))
    for ref, first in ((ylo_ref, 0), (yhi_ref, wy - 2)):
        for x in range(wx):
            ref[pl.ds(x * pair, pair), :] = jnp.concatenate(
                [sp_ref[pl.ds(x * wy + first + k, kinds, stride=step), :] for k in range(2)],
                axis=0,
            ).astype(bf16)
        base = wx * pair
        for k in range(2):
            high, low = split(kappa_ref[pl.ds(first + k, wx, stride=wy), :])
            ref[pl.ds(base + k * wx, wx), :] = high
            ref[pl.ds(base + (2 + k) * wx, wx), :] = low
        high, low = split(vel_ref[pl.ds(rows + first, wx, stride=wy), :])
        ref[pl.ds(base + 4 * wx, wx), :] = high
        ref[pl.ds(base + 5 * wx, wx), :] = low


def own_planes(sp_ref, kappa_ref, vel_ref, grid_ref, xlo_ref, xhi_ref, wx, wy, kinds):
    rows = wx * wy
    pair = 2 * kinds

    @pl.loop(0, wx)
    def _(x):
        for start in range(0, wy, BATCH):
            ys = range(start, start + BATCH)
            lines = [sp_ref[pl.ds(x * wy + y, kinds, stride=rows + GAP), :] for y in ys]
            for y, line in zip(ys, lines):
                grid_ref[x * wy + y] = line

    def cell(x, y):
        return grid_ref[x * wy + y]

    for ref, planes in ((xlo_ref, (0, 1)), (xhi_ref, (wx - 1, wx - 2))):
        for k, x in enumerate(planes):
            for y in range(0, wy, 2):
                ref[pl.ds(k * wy * kinds + y * kinds, pair), :] = jnp.concatenate(
                    [cell(x, y), cell(x, y + 1)], axis=0
                ).astype(bf16)
        base = 2 * wy * kinds
        for k, x in enumerate(planes):
            high, low = split(kappa_ref[pl.ds(x * wy, wy), :])
            ref[pl.ds(base + k * wy, wy), :] = high
            ref[pl.ds(base + (2 + k) * wy, wy), :] = low
        high, low = split(vel_ref[pl.ds(planes[0] * wy, wy), :])
        ref[pl.ds(base + 4 * wy, wy), :] = high
        ref[pl.ds(base + 5 * wy, wy), :] = low


def prepare_kernel(
    count_ref,
    index_hbm,
    before_hbm,
    beforet_hbm,
    upper_hbm,
    sp_hbm,
    kappa_hbm,
    vel_hbm,
    grid_ref,
    xlo_ref,
    xhi_ref,
    table_hbm,
    place_hbm,
    offset_hbm,
    table_ref,
    place_ref,
    offset_ref,
    sp_pad,
    kappa_ref,
    vel_ref,
    index_ref,
    before_ref,
    beforet_ref,
    upper_ref,
    onerow,
    onecol,
    sems,
    *,
    wx,
    wy,
    kinds,
):
    copies = start_all(
        [
            (index_hbm, index_ref),
            (before_hbm, before_ref),
            (beforet_hbm, beforet_ref),
            (upper_hbm, upper_ref),
            (kappa_hbm, kappa_ref),
            (vel_hbm, vel_ref),
        ]
        + load_species(sp_hbm, sp_pad, wx * wy),
        sems,
    )
    wait_all(copies[:4])
    list_kernel(
        count_ref,
        index_ref,
        before_ref,
        beforet_ref,
        upper_ref,
        table_ref,
        place_ref,
        offset_ref,
        onerow,
        onecol,
        rows=wx * wy,
    )
    wait_all(copies[4:])
    outs = start_all(
        [(offset_ref, offset_hbm), (table_ref, table_hbm), (place_ref, place_hbm)], sems
    )
    own_planes(as_lines(sp_pad), kappa_ref, vel_ref, grid_ref, xlo_ref, xhi_ref, wx, wy, kinds)
    wait_all(outs)


def x_message_kernel(yprev, ynext, ownlo_ref, ownhi_ref, xlo_ref, xhi_ref, *, wx, wy, kinds):
    own = ownlo_ref.shape[0]
    pair = 2 * kinds
    ybase = wx * pair
    xlo_ref[pl.ds(0, own), :] = ownlo_ref[...]
    xhi_ref[pl.ds(0, own), :] = ownhi_ref[...]
    for ref, x in ((xlo_ref, 0), (xhi_ref, wx - 1)):
        at = own
        for halo, k in ((yprev, 1), (ynext, 0)):
            ref[pl.ds(at, pair), :] = halo[pl.ds(x * pair, pair), :]
            at += pair
            for part in (k, 2 + k):
                ref[pl.ds(at, wx), :] = halo[pl.ds(ybase + part * wx, wx), :]
                at += wx


def list_kernel(count_ref, index_ref, before_ref, beforet_ref, upper_ref, table_ref, place_ref, offset_ref, onerow, onecol, *, rows):
    count = count_ref[0]
    capacity = index_ref.shape[1]
    step = 512
    parts = capacity // step

    def parts_of(j):
        number = index_ref[:, pl.ds(j * step, step)]
        valid = (lax.broadcasted_iota(jnp.int32, (1, step), 1) + j * step) < count
        row = jnp.where(valid, number // LANES, -1)
        return row, number % LANES, valid

    mask = jnp.zeros((rows, LANES), f32)
    for j in range(parts):
        row, col, valid = parts_of(j)
        hit = lax.broadcasted_iota(jnp.int32, (rows, step), 0) == row
        onerow[:, j * step : (j + 1) * step] = hit.astype(f32).astype(bf16)
        hit = lax.broadcasted_iota(jnp.int32, (LANES, step), 0) == col
        onecol[:, j * step : (j + 1) * step] = hit.astype(f32).astype(bf16)
    mask = dot_nt(onerow[...], onecol[...])
    maskb = mask.astype(bf16)
    rank = dot(maskb, upper_ref[...])
    total = dot(maskb, jnp.ones((LANES, LANES), bf16))
    offset = dot(before_ref[...], total.astype(bf16))
    total_row = dot_nt(jnp.ones((8, LANES), bf16), maskb)
    offset_ref[...] = dot(total_row.astype(bf16), beforet_ref[...]).astype(jnp.int32)
    place = (offset + rank).astype(jnp.int32)
    place_hi = (place // LANES).astype(f32)
    place_lo = (place % LANES).astype(f32)
    place_ref[...] = jnp.where(mask > 0.5, place % LANES, place % LANES - LANES)
    both = jnp.concatenate([place_hi.T, place_lo.T], axis=0).astype(bf16)
    table = jnp.zeros(table_ref.shape, f32)
    for j in range(parts):
        row, col, valid = parts_of(j)
        found = dot(both, onerow[:, j * step : (j + 1) * step])
        colf = onecol[:, j * step : (j + 1) * step].astype(f32)
        hi = jnp.sum(found[:LANES] * colf, axis=0, keepdims=True)
        lo = jnp.sum(found[LANES:] * colf, axis=0, keepdims=True)
        hi = jnp.where(valid, hi, -1.0).astype(jnp.int32)
        lo = lo.astype(jnp.int32)
        put_hi = jnp.where(
            lax.broadcasted_iota(jnp.int32, (table_ref.shape[0], step), 0) == hi,
            col.astype(f32),
            0.0,
        ).astype(bf16)
        put_lo = (
            (lax.broadcasted_iota(jnp.int32, (LANES, step), 0) == lo).astype(f32).astype(bf16)
        )
        table = table + dot_nt(put_hi, put_lo)
    table_ref[...] = table.astype(jnp.int32)


def make_weights(kp, we, wn, wu, wd, ws, wx):
    scale = 0.5 * diffuse_step

    def line(px):
        base = px * PADK
        here = kp[pl.ds(base, PADK), :]
        up = jnp.roll(here, -1, 1)
        wu_v = scale * (here + up)
        we_v = scale * (here + kp[pl.ds(base + PADK, PADK), :])
        wn_v = scale * (here + kp[pl.ds(base + 1, PADK), :])
        ww_v = scale * (here + kp[pl.ds(base - PADK, PADK), :])
        wsouth = scale * (here + kp[pl.ds(base - 1, PADK), :])
        wd_v = jnp.roll(wu_v, 1, 1)
        we[pl.ds(base, PADK), :] = we_v
        wn[pl.ds(base, PADK), :] = wn_v
        wu[pl.ds(base, PADK), :] = wu_v
        wd[pl.ds(base, PADK), :] = wd_v
        ws[pl.ds(base, PADK), :] = ((we_v + ww_v) + (wn_v + wsouth)) + (wu_v + wd_v)

    for px in range(1, wx + 3):
        line(px)
    base = 0
    here = kp[pl.ds(base, PADK), :]
    we[pl.ds(base, PADK), :] = scale * (here + kp[pl.ds(base + PADK, PADK), :])


def cell_update(src, row, line, px, py, weights, lewis):
    we, wn, wu, wd, ws = weights
    kr = px * PADK + py

    def w(ref, r):
        return ref[pl.ds(r, 1), :]

    here = src[row]
    total = w(we, kr) * src[row + line] + w(we, kr - PADK) * src[row - line]
    total = total + (w(wn, kr) * src[row + 1] + w(wn, kr - 1) * src[row - 1])
    total = total + (w(wu, kr) * jnp.roll(here, -1, 1) + w(wd, kr) * jnp.roll(here, 1, 1))
    total = total - w(ws, kr) * here
    return here + lewis * total


def pad_row(px, py):
    return px * PADW + py


def update_cells(src, dst, cells, src_row, dst_row, line, weights, lewis):
    for start in range(0, len(cells), 4):
        part = cells[start : start + 4]
        values = [cell_update(src, src_row(px, py), line, px, py, weights, lewis) for px, py in part]
        for (px, py), value in zip(part, values):
            dst[dst_row(px, py)] = value


def column(scalars, kinds):
    row = lax.broadcasted_iota(jnp.int32, (kinds, LANES), 0)
    value = jnp.full((kinds, LANES), scalars[0], f32)
    for s in range(1, kinds):
        value = jnp.where(row == s, scalars[s], value)
    return value


def fill_own(kp, kappa_ref, wx, wy):
    for x in range(wx):
        kp[pl.ds((x + 2) * PADK + 2, wy), :] = kappa_ref[pl.ds(x * wy, wy), :]


def collect(listed, p2, table_ref, offset_s, compact, kinds):
    lane = lax.broadcasted_iota(jnp.int32, (1, LANES), 1)
    for start in range(0, len(listed), BATCH):
        ready = []
        for r in listed[start : start + BATCH]:
            offset = offset_s[0, r]
            hi = offset // LANES
            later = lane >= offset % LANES
            pick = jnp.where(later, table_ref[pl.ds(hi, 1), :], table_ref[pl.ds(hi + 1, 1), :])
            got = jnp.take_along_axis(
                p2[r], jnp.broadcast_to(pick, (kinds, LANES)), axis=1, mode="promise_in_bounds"
            )
            ready.append((hi, later, got))
        for hi, later, got in ready:
            pltpu.store(compact.at[hi], got, mask=jnp.broadcast_to(later, (kinds, LANES)))
            compact[hi + 1] = got


def spread(r, rates, place_ref, offset_s, kinds):
    lane = lax.broadcasted_iota(jnp.int32, (1, LANES), 1)
    offset = offset_s[0, r]
    hi = offset // LANES
    lo = offset % LANES
    merged = jnp.where(jnp.broadcast_to(lane >= lo, (kinds, LANES)), rates[hi], rates[hi + 1])
    place = place_ref[pl.ds(r, 1), :]
    live = jnp.broadcast_to(place >= 0, (kinds, LANES))
    pick = jnp.broadcast_to(place & (LANES - 1), (kinds, LANES))
    got = jnp.take_along_axis(merged, pick, axis=1, mode="promise_in_bounds")
    return jnp.where(live, got, 0.0)


def network_tile(t, compact, rates, w1_ref, w2_ref, w3_ref, w4_ref):
    blocks = TILE // LANES
    cells = jnp.concatenate([compact[t * blocks + k] for k in range(blocks)], axis=1)
    hidden = silu(dot(w1_ref[...], cells.astype(bf16))).astype(bf16)
    hidden = silu(dot(w2_ref[...], hidden)).astype(bf16)
    hidden = silu(dot(w3_ref[...], hidden)).astype(bf16)
    result = dot(w4_ref[...], hidden).astype(bf16).astype(f32)
    for k in range(blocks):
        rates[t * blocks + k] = result[:, k * LANES : (k + 1) * LANES]


def inner_kernel(
    lewis_s,
    after_ref,
    p0,
    kappa_hbm,
    table_hbm,
    offset_hbm,
    w1_hbm,
    w2_hbm,
    w3_hbm,
    w4_hbm,
    p1_hbm,
    p2_hbm,
    compact_hbm,
    rates_hbm,
    p1,
    p2,
    compact,
    rates,
    kappa_ref,
    table_ref,
    w1_ref,
    w2_ref,
    w3_ref,
    w4_ref,
    kp,
    we,
    wn,
    wu,
    wd,
    ws,
    offset_s,
    sems,
    *,
    wx,
    wy,
    kinds,
):
    copies = start_all(
        [
            (kappa_hbm, kappa_ref),
            (offset_hbm, offset_s),
            (table_hbm, table_ref),
            (w1_hbm, w1_ref),
            (w2_hbm, w2_ref),
            (w3_hbm, w3_ref),
            (w4_hbm, w4_ref),
        ],
        sems,
    )
    weights = (we, wn, wu, wd, ws)
    lewis = 1.0 / column(lewis_s, kinds)
    copies[0].wait()
    fill_own(kp, kappa_ref, wx, wy)
    make_weights(kp, we, wn, wu, wd, ws, wx)

    def row_of(px, py):
        return (px - 2) * wy + py - 2

    @pl.loop(3, wx + 1)
    def _(px):
        cells = [(px, py) for py in range(3, wy + 1)]
        update_cells(p0, p1, cells, row_of, row_of, wy, weights, lewis)

    @pl.loop(4, wx)
    def _(px):
        cells = [(px, py) for py in range(4, wy)]
        update_cells(p1, p2, cells, row_of, row_of, wy, weights, lewis)

    wait_all(copies[1:])

    @pl.loop(2, wx - 2)
    def _(x):
        listed = [x * wy + y for y in range(2, wy - 2)]
        collect(listed, p2, table_ref, offset_s, compact, kinds)

    outs = start_all([(p1, p1_hbm), (p2, p2_hbm), (compact, compact_hbm)], sems)

    @pl.loop(0, offset_s[0, 0] // TILE)
    def _(t):
        network_tile(t, compact, rates, w1_ref, w2_ref, w3_ref, w4_ref)

    wait_all(outs)
    wait_all(start_all([(rates, rates_hbm)], sems))


def ring_copies(src, dst, wx, wy, inset):
    pairs = []
    wide_x = (inset, wx - 2 * inset)
    wide_y = (inset, wy - 2 * inset)
    for xs, ys in (
        ((inset, 2), wide_y),
        ((wx - inset - 2, 2), wide_y),
        (wide_x, (inset, 2)),
        (wide_x, (wy - inset - 2, 2)),
    ):
        if ys[1] == 2:
            xs = (xs[0] + 2, xs[1] - 4)
        pairs.append(
            (
                src.at[pl.ds(*xs), pl.ds(*ys)],
                dst.at[pl.ds(xs[0] + 2, xs[1]), pl.ds(ys[0] + 2, ys[1])],
            )
        )
    return pairs


def outer_kernel(
    count_ref,
    heat_s,
    lewis_s,
    yprev_ref,
    ynext_ref,
    xprev_ref,
    xnext_ref,
    zmat_hbm,
    grid_hbm,
    p1_hbm,
    inner_hbm,
    compact_hbm,
    rates_hbm,
    kappa_hbm,
    vel_hbm,
    table_hbm,
    place_hbm,
    offset_hbm,
    w1_hbm,
    w2_hbm,
    w3_hbm,
    w4_hbm,
    out_ref,
    p2_hbm,
    rates_out,
    pad0,
    pad1,
    slab2,
    compact,
    rates,
    kappa_ref,
    vel_ref,
    table_ref,
    place_ref,
    zmat_ref,
    w1_ref,
    w2_ref,
    w3_ref,
    w4_ref,
    kp,
    we,
    wn,
    wu,
    wd,
    ws,
    heat_slots,
    heat_rows,
    offset_s,
    sems,
    ring_sems,
    *,
    wx,
    wy,
    kinds,
):
    rings = start_all(
        ring_copies(grid_hbm, pad0, wx, wy, 0) + ring_copies(p1_hbm, pad1, wx, wy, 1), ring_sems
    )
    p0 = as_lines(pad0)
    p1 = as_lines(pad1)
    p2 = as_lines(slab2)
    mid = (pl.ds(2, wx - 4), pl.ds(2, wy - 4))
    copies = start_all(
        [
            (kappa_hbm, kappa_ref),
            (offset_hbm, offset_s),
            (table_hbm, table_ref),
            (compact_hbm, compact),
            (rates_hbm, rates),
            (w1_hbm, w1_ref),
            (w2_hbm, w2_ref),
            (w3_hbm, w3_ref),
            (w4_hbm, w4_ref),
            (place_hbm, place_ref),
            (vel_hbm, vel_ref),
            (zmat_hbm, zmat_ref),
            (inner_hbm.at[mid], slab2.at[mid]),
        ],
        sems,
    )
    rows = wx * wy
    pair = 2 * kinds
    weights = (we, wn, wu, wd, ws)
    lewis = 1.0 / column(lewis_s, kinds)
    wait_all(copies[:1])
    fill_own(kp, kappa_ref, wx, wy)
    ybase = wx * pair
    for ref, py in ((yprev_ref, 0), (ynext_ref, wy + 2)):
        for x in range(wx):
            both = ref[pl.ds(x * pair, pair), :].astype(f32)
            p0[(x + 2) * PADW + py] = both[:kinds]
            p0[(x + 2) * PADW + py + 1] = both[kinds:]
        for k in range(2):
            value = ref[pl.ds(ybase + k * wx, wx), :].astype(f32) + ref[
                pl.ds(ybase + (2 + k) * wx, wx), :
            ].astype(f32)
            kp[pl.ds(2 * PADK + py + k, wx, stride=PADK), :] = value
    xbase = 2 * wy * kinds
    cbase = xbase + 6 * wy
    for ref, near, far, edge in ((xprev_ref, 1, 0, wx - 1), (xnext_ref, wx + 2, wx + 3, 0)):
        for k, px in ((0, near), (1, far)):
            for y in range(0, wy, 2):
                both = ref[pl.ds(k * wy * kinds + y * kinds, pair), :].astype(f32)
                p0[px * PADW + y + 2] = both[:kinds]
                p0[px * PADW + y + 3] = both[kinds:]
            value = ref[pl.ds(xbase + k * wy, wy), :].astype(f32) + ref[
                pl.ds(xbase + (2 + k) * wy, wy), :
            ].astype(f32)
            kp[pl.ds(px * PADK + 2, wy), :] = value
        piece = pair + 2 * wx
        for k, py in ((0, 1), (1, wy + 2)):
            start = cbase + k * piece
            both = ref[pl.ds(start, pair), :].astype(f32)
            p0[near * PADW + py] = both[kinds:] if k == 0 else both[:kinds]
            value = ref[pl.ds(start + pair, wx), :].astype(f32) + ref[
                pl.ds(start + pair + wx, wx), :
            ].astype(f32)
            kp[pl.ds(near * PADK + py, 1), :] = value[edge : edge + 1]
    make_weights(kp, we, wn, wu, wd, ws, wx)

    def second_row(px, py):
        return (px - 2) * wy + py - 2

    wait_all(rings)

    def first(cells):
        update_cells(p0, p1, cells, pad_row, pad_row, PADW, weights, lewis)

    def second(cells):
        update_cells(p1, p2, cells, pad_row, second_row, PADW, weights, lewis)

    @pl.loop(0, 2)
    def _(k):
        first([(1 + k * (wx + 1), py) for py in range(2, wy + 2)])
        first([(2 + k * (wx - 1), py) for py in range(1, wy + 3)])

    @pl.loop(3, wx + 1)
    def _(px):
        first([(px, py) for py in (1, 2, wy + 1, wy + 2)])

    @pl.loop(0, 2)
    def _(k):
        second([(2 + k * (wx - 2), py) for py in range(2, wy + 2)])
        second([(3 + k * (wx - 2), py) for py in range(2, wy + 2)])

    @pl.loop(4, wx)
    def _(px):
        second([(px, py) for py in (2, 3, wy, wy + 1)])

    wait_all(copies[1:])
    outs = start_all([(slab2, p2_hbm)], ring_sems)

    def take(listed):
        collect(listed, p2, table_ref, offset_s, compact, kinds)

    @pl.loop(0, 2)
    def _(x):
        take([x * wy + y for y in range(wy)])

    @pl.loop(0, (wx - 4) // 2)
    def _(k):
        edge = (0, 1, wy - 2, wy - 1)
        take([(2 + 2 * k + i) * wy + y for i in range(2) for y in edge])

    @pl.loop(wx - 2, wx)
    def _(x):
        take([x * wy + y for y in range(wy)])

    count = count_ref[0]

    @pl.loop(offset_s[0, 0] // TILE, (count + TILE - 1) // TILE)
    def _(t):
        network_tile(t, compact, rates, w1_ref, w2_ref, w3_ref, w4_ref)

    wait_all(outs)
    outs = start_all([(rates, rates_out)], ring_sems)
    release = column(heat_s, kinds)
    for k in range(heat_slots.shape[0] // BATCH):
        heat_slots[pl.ds(k * BATCH, BATCH), :] = jnp.concatenate(
            [
                jnp.sum(release * rates[k * BATCH + i], axis=0, keepdims=True)
                for i in range(BATCH)
            ],
            axis=0,
        )
    lane = lax.broadcasted_iota(jnp.int32, (1, LANES), 1)

    @pl.loop(0, rows // BATCH)
    def _(k):
        lines = []
        for i in range(BATCH):
            offset = offset_s[0, k * BATCH + i]
            hi = offset // LANES
            later = lane >= offset % LANES
            lines.append(
                jnp.where(later, heat_slots[pl.ds(hi, 1), :], heat_slots[pl.ds(hi + 1, 1), :])
            )
        at = pl.ds(pl.multiple_of(k * BATCH, BATCH), BATCH)
        place = place_ref[at, :]
        got = jnp.take_along_axis(
            jnp.concatenate(lines, axis=0),
            place & (LANES - 1),
            axis=1,
            mode="promise_in_bounds",
        )
        heat_rows[at, :] = jnp.where(place >= 0, got, 0.0)

    ux = vel_ref[pl.ds(0, rows), :]
    nextx = xnext_ref[pl.ds(xbase + 4 * wy, wy), :].astype(f32) + xnext_ref[
        pl.ds(xbase + 5 * wy, wy), :
    ].astype(f32)
    east = jnp.concatenate([ux[wy:], nextx], axis=0)
    nexty = ynext_ref[pl.ds(ybase + 4 * wx, wx), :].astype(f32) + ynext_ref[
        pl.ds(ybase + 5 * wx, wx), :
    ].astype(f32)
    uy = vel_ref[pl.ds(rows, rows), :]
    north = vel_ref[pl.ds(rows + 1, rows), :]
    last = lax.broadcasted_iota(jnp.int32, (wy, LANES), 0) == wy - 1
    pieces = []
    for x in range(wx):
        pieces.append(
            jnp.where(
                last,
                jnp.broadcast_to(nexty[x : x + 1], (wy, LANES)),
                north[x * wy : (x + 1) * wy],
            )
        )
    north = jnp.concatenate(pieces, axis=0)
    uz = vel_ref[pl.ds(2 * rows, rows), :]
    source = (east - ux) + (north - uy) + (jnp.roll(uz, -1, 1) - uz) - heat_rows[...]
    turned = jnp.concatenate(
        [source[h * LANES : (h + 1) * LANES].T for h in range(rows // LANES)], axis=0
    )
    out_ref[...] = dot(zmat_ref[...], turned, HIGHEST)
    wait_all(outs)


def species_kernel(
    qy_hbm,
    qyt_hbm,
    bx_hbm,
    bxt_hbm,
    pick_hbm,
    kind_hbm,
    inv_hbm,
    p2_hbm,
    rates_hbm,
    place_hbm,
    offset_hbm,
    spec_hbm,
    qy_ref,
    qyt_ref,
    bx_ref,
    bxt_ref,
    pick_ref,
    kind_ref,
    inv_ref,
    p2,
    rates,
    place_ref,
    offset_s,
    stage,
    sems,
    in_sems,
    out_sems,
    *,
    wx,
    wy,
    kinds,
):
    rows = wx * wy
    parts = in_sems.shape[0]
    size = rows // parts
    first = start_all([(offset_hbm, offset_s), (place_hbm, place_ref), (rates_hbm, rates)], sems)
    chunks = [pl.ds(c * size, size) for c in range(parts)]
    loads = start_all([(p2_hbm.at[c], p2.at[c]) for c in chunks], in_sems)
    tables = [
        pltpu.make_async_copy(a, b, sems.at[3 + k])
        for k, (a, b) in enumerate(
            [
                (qy_hbm, qy_ref),
                (qyt_hbm, qyt_ref),
                (bx_hbm, bx_ref),
                (bxt_hbm, bxt_ref),
                (pick_hbm, pick_ref),
                (kind_hbm, kind_ref),
                (inv_hbm, inv_ref),
            ]
        )
    ]
    for copy in tables:
        copy.start()
    lines_out = as_lines(stage)
    wait_all(first)
    stores = []
    for c in range(parts):
        loads[c].wait()

        @pl.loop(c * size // BATCH, (c + 1) * size // BATCH)
        def _(k):
            lines = []
            for i in range(BATCH):
                r = k * BATCH + i
                lines.append(p2[r] + react_step * spread(r, rates, place_ref, offset_s, kinds))
            for i in range(BATCH):
                lines_out[pl.ds(k * BATCH + i, kinds, stride=rows + GAP), :] = lines[i]

        copy = pltpu.make_async_copy(
            stage.at[:, chunks[c]], spec_hbm.at[:, chunks[c]], out_sems.at[c]
        )
        copy.start()
        stores.append(copy)
    wait_all(tables + stores)


def solve_kernel(
    in_ref, lam_ref, lamy_ref, qy_ref, qyt_ref, bx_ref, bxt_ref, pick_ref, kind_ref, out_ref, lines, tiles, *, na, nb, wide, keep
):
    groups = LANES // wide
    spans = nb // groups
    lane = lax.broadcasted_iota(jnp.int32, (1, LANES), 1) // wide
    for a in range(na):
        for span in range(spans):
            blocks = [
                in_ref[pl.ds((a * nb + span * groups + g) * keep, keep), :] for g in range(groups)
            ]
            for g in range(groups):
                line = blocks[g]
                for b in range(groups):
                    if b != g:
                        moved = pltpu.roll(blocks[b], ((b - g) * wide) % LANES, 1)
                        line = jnp.where(lane == b, moved, line)
                lines[pl.ds((g * na + a) * keep, keep), span * LANES : (span + 1) * LANES] = line
    wave = dot(bx_ref[...], dot(lines[...], qyt_ref[...], HIGHEST), HIGHEST)
    lam = lam_ref[...] + lamy_ref[...]
    anchor = lam == 0.0
    wave = jnp.where(anchor, 0.0, wave / jnp.where(anchor, 1.0, lam))
    lines[...] = dot(dot(bxt_ref[...], wave, HIGHEST), qy_ref[...], HIGHEST)
    for a in range(na):
        for span in range(spans):
            blocks = [
                lines[pl.ds((g * na + a) * keep, keep), span * LANES : (span + 1) * LANES]
                for g in range(groups)
            ]
            for b in range(groups):
                tile = blocks[b]
                for g in range(groups):
                    if b != g:
                        moved = pltpu.roll(blocks[g], ((g - b) * wide) % LANES, 1)
                        tile = jnp.where(lane == g, moved, tile)
                where = a * nb + span * groups + b
                tiles[pl.ds(where * keep, keep), :] = tile
                out_ref[pl.ds(where * (keep + 1), keep), :] = tile
    south_pick = pick_ref[pl.ds(0, keep), :]
    west_pick = pick_ref[pl.ds(keep, keep), :]
    kind = kind_ref[...]
    for a in range(na):
        for b in range(nb):
            south = tiles[pl.ds((a * nb + (b - 1) % nb) * keep, keep), :]
            west = tiles[pl.ds(((a - 1) % na * nb + b) * keep, keep), :]
            south = jnp.take_along_axis(south, south_pick, axis=1, mode="promise_in_bounds")
            west = jnp.take_along_axis(west, west_pick, axis=1, mode="promise_in_bounds")
            both = jnp.where(kind == 1, south, jnp.where(kind == 2, west, 0.0))
            out_ref[pl.ds((a * nb + b) * (keep + 1) + keep, 1), :] = jnp.sum(
                both, axis=0, keepdims=True
            )


def slope_kernel(in_ref, inv_ref, vel_ref, out_ref, padded, extra, field, *, wx, wy, modes):
    rows = wx * wy
    halves = rows // LANES
    total = in_ref.shape[0]
    full = padded.shape[0]
    padded[pl.ds(0, total), :] = in_ref[...]
    if full > total:
        padded[pl.ds(total, full - total), :] = jnp.zeros((full - total, LANES), f32)
    turned = jnp.concatenate(
        [padded[pl.ds(k * LANES, LANES), :].T for k in range(full // LANES)], axis=1
    )
    wave = dot(turned, inv_ref[...], HIGHEST)
    for h in range(halves):
        field[pl.ds(wy + h * LANES, LANES), :] = wave[:, h * LANES : (h + 1) * LANES]
    for m in range(modes):
        extra[m] = wave[:, (halves + m) * LANES : (halves + m + 1) * LANES]
    south = []
    west = []
    lines = LANES // wy
    for h in range(halves):
        south.append(sum(extra[m, pl.ds(h * modes + m, lines, stride=wy), :] for m in range(modes)))
    for g in range(2):
        west.append(sum(extra[m, pl.ds((m * 2 + g) * wy + wy // 2, wy // 2), :] for m in range(modes)))
    field[pl.ds(0, wy), :] = jnp.concatenate(west, axis=0)
    here = field[pl.ds(wy, rows), :]
    out_ref[pl.ds(0, rows), :] = vel_ref[pl.ds(0, rows), :] - (here - field[pl.ds(0, rows), :])
    first = lax.broadcasted_iota(jnp.int32, (wy, LANES), 0) == 0
    for x in range(wx):
        behind = field[pl.ds(wy - 1 + x * wy, wy), :]
        edge = south[x // lines][x % lines : x % lines + 1]
        behind = jnp.where(first, jnp.broadcast_to(edge, (wy, LANES)), behind)
        at = pl.ds(rows + x * wy, wy)
        out_ref[at, :] = vel_ref[at, :] - (here[x * wy : (x + 1) * wy] - behind)
    at = pl.ds(2 * rows, rows)
    out_ref[at, :] = vel_ref[at, :] - (here - jnp.roll(here, 1, 1))


def real_basis(n):
    at = np.arange(n)
    basis = np.zeros((n, n))
    waves = np.zeros(n, dtype=np.int64)
    basis[0] = 1.0 / np.sqrt(n)
    for k in range(1, (n + 1) // 2):
        angle = 2.0 * np.pi * ((k * at) % n) / n
        basis[2 * k - 1] = np.sqrt(2.0 / n) * np.cos(angle)
        basis[2 * k] = np.sqrt(2.0 / n) * np.sin(angle)
        waves[2 * k - 1] = k
        waves[2 * k] = k
    if n % 2 == 0:
        basis[n - 1] = np.where(at % 2 == 0, 1.0, -1.0) / np.sqrt(n)
        waves[n - 1] = n // 2
    return basis, -4.0 * np.sin(np.pi * waves / n) ** 2


@functools.lru_cache(maxsize=None)
def plan(wx, wy, depth, na, nb):
    rows = wx * wy
    halves = rows // LANES
    devices = na * nb
    modes = depth // devices
    keep = halves * modes
    lines = LANES // wy
    zb, lamz = real_basis(depth)
    qx, lamx = real_basis(wx * na)
    qy, lamy = real_basis(wy * nb)
    zmat = np.zeros((devices, halves, modes, halves, depth))
    for h in range(halves):
        zmat[:, h, :, h, :] = zb.reshape(devices, modes, depth)
    zmat = zmat.reshape(devices * keep, halves * depth)
    inv = np.zeros((devices, keep + 1, halves + modes, depth))
    for h in range(halves):
        for m in range(modes):
            inv[:, h * modes + m, h, :] = zb.reshape(devices, modes, depth)[:, m]
    for m in range(modes):
        inv[:, keep, halves + m, :] = zb.reshape(devices, modes, depth)[:, m]
    inv = inv.reshape(devices * (keep + 1), (halves + modes) * depth)
    full = -(-inv.shape[0] // LANES) * LANES
    inv = np.pad(inv, ((0, full - inv.shape[0]), (0, 0)))
    bx = np.zeros((wx * na, modes, lines, na, halves, modes))
    for g in range(lines):
        for a in range(na):
            for h in range(halves):
                for m in range(modes):
                    bx[:, m, g, a, h, m] = qx[:, a * wx + h * lines + g]
    bx = bx.reshape(wx * na * modes, lines * na * keep)
    pick = np.zeros((2, keep, LANES), np.int32)
    kind = np.zeros((keep, LANES), np.int32)
    for k in range(keep):
        for g in range(lines):
            pick[0, k, g * wy + k] = g * wy + wy - 1
            kind[k, g * wy + k] = 1
    for m in range(modes):
        for y in range(wy):
            to = (m * 2 + y // (wy // 2)) * wy + wy // 2 + y % (wy // 2)
            pick[1, (halves - 1) * modes + m, to] = LANES - wy + y
            kind[(halves - 1) * modes + m, to] = 2
    inner = [
        x * wy + y for x in range(wx) for y in range(wy) if 2 <= x < wx - 2 and 2 <= y < wy - 2
    ]
    outer = [r for r in range(rows) if r not in set(inner)]
    order = np.array(inner + outer)
    turn = np.empty(rows, np.int64)
    turn[order] = np.arange(rows)
    before = turn[None, :] < turn[:, None]
    upper = np.arange(LANES)[:, None] < np.arange(LANES)[None, :]
    as32 = lambda v: np.asarray(v, np.float32)
    as16 = lambda v: np.asarray(v, np.float32).astype(jnp.bfloat16)
    return dict(
        zmat=as32(zmat),
        inv=as32(inv),
        bx=as32(bx),
        bxt=as32(bx.T),
        qy=as32(qy),
        qyt=as32(qy.T),
        lamx=as32(np.repeat(lamx, modes)[:, None]),
        lamy=as32(lamy[None, :]),
        lamz=as32(lamz),
        pick=pick.reshape(2 * keep, LANES),
        kind=kind,
        order=order.astype(np.int32),
        before=as16(before),
        beforet=as16(before.T),
        upper=as16(upper),
        inner=len(inner),
    )


def shift(value, axis, by):
    peers = lax.axis_size(axis)
    return lax.ppermute(value, axis, [(i, (i + by) % peers) for i in range(peers)])


def params(megabytes):
    return pltpu.CompilerParams(vmem_limit_bytes=megabytes * 2**20)


def per_device(
    species,
    diffusivity,
    lewis_number,
    velocity,
    layer_one,
    layer_two,
    layer_three,
    layer_four,
    heat_release,
    react_index,
    react_count,
):
    kinds, wx, wy, depth = species.shape
    na = lax.axis_size("gx")
    nb = lax.axis_size("gy")
    devices = na * nb
    rows = wx * wy
    halves = rows // LANES
    modes = depth // devices
    keep = halves * modes
    tab = plan(wx, wy, depth, na, nb)
    sp = species.reshape(kinds * rows, depth)
    kappa = diffusivity.reshape(rows, depth)
    vel = velocity.reshape(3 * rows, depth)
    count = react_count.reshape(1)
    capacity = react_index.size
    slots = capacity // LANES
    sds = jax.ShapeDtypeStruct
    own = 2 * wy * kinds + 6 * wy

    def call(body, outs, ins, scratch, name, megabytes, flops, aliases=None, out_specs=None):
        return pl.pallas_call(
            body,
            out_shape=outs,
            in_specs=ins,
            out_specs=out_specs or [spec_vmem()] * len(outs),
            scratch_shapes=scratch,
            input_output_aliases=aliases or {},
            compiler_params=params(megabytes),
            cost_estimate=pl.CostEstimate(flops=flops, bytes_accessed=2**20, transcendentals=0),
            name=name,
        )

    def same(array):
        return sds(array.shape, array.dtype)

    def dma(n):
        return pltpu.SemaphoreType.DMA((n,))

    sizes = dict(wx=wx, wy=wy, kinds=kinds)
    def vmem(shape, dtype=f32):
        return pltpu.VMEM(shape, dtype)

    message = sds((own, depth), bf16)
    padded_species = vmem((kinds, rows + GAP, depth))
    sp3 = sp.reshape(kinds, rows, depth)
    own_lines = [padded_species, vmem(kappa.shape), vmem(vel.shape)]
    ylo, yhi = call(
        functools.partial(y_message_kernel, **sizes),
        [message] * 2,
        [spec_hbm()] * 3,
        own_lines + [dma(3)],
        "ymessage",
        52,
        10**7,
    )(sp3, kappa, vel)

    yprev = shift(yhi, "gy", 1)
    ynext = shift(ylo, "gy", -1)

    index = react_index.reshape(1, capacity)
    layers = (layer_one, layer_two, layer_three, layer_four)
    lists = (index, tab["before"], tab["beforet"], tab["upper"])
    table_t = sds((slots + 8, LANES), jnp.int32)
    place_t = sds((rows, LANES), jnp.int32)
    offset_t = sds((8, rows), jnp.int32)
    lines_t = sds((rows, kinds, depth), f32)
    grid, xlo, xhi, table, place, offset = call(
        functools.partial(prepare_kernel, **sizes),
        [lines_t, message, message, table_t, place_t, offset_t],
        [spec_smem()] + [spec_hbm()] * 7,
        [vmem(v.shape, v.dtype) for v in (table_t, place_t, offset_t)]
        + own_lines
        + [vmem(v.shape, v.dtype) for v in lists]
        + [vmem((rows, capacity), bf16), vmem((LANES, capacity), bf16), dma(7)],
        "prepare",
        52,
        5 * 10**9,
        out_specs=[spec_vmem()] * 3 + [spec_hbm()] * 3,
    )(count, *lists, sp3, kappa, vel)

    extra = 2 * (2 * kinds + 2 * wx)
    message = sds((own + extra, depth), bf16)
    xlo, xhi = call(
        functools.partial(x_message_kernel, **sizes),
        [message, message],
        [spec_vmem()] * 4,
        [],
        "xmessage",
        52,
        10**7,
    )(yprev, ynext, xlo, xhi)
    xprev = shift(xhi, "gx", 1)
    xnext = shift(xlo, "gx", -1)

    weight_rows = [vmem((PADW * PADK + 8, depth))] * 6
    layers_v = [vmem(w.shape, w.dtype) for w in layers]
    compacted = sds((slots + 8, kinds, LANES), f32)
    lewis = lewis_number
    release = heat_release
    cells4 = (wx, wy, kinds, depth)
    smem = pltpu.SMEM((8, rows), jnp.int32)
    lines_v = vmem(lines_t.shape)
    compact_v = vmem(compacted.shape)
    p1, p2, compact, rates = call(
        functools.partial(inner_kernel, **sizes),
        [lines_t, lines_t, compacted, compacted],
        [spec_smem(), spec_any(), spec_vmem()] + [spec_hbm()] * 7,
        [lines_v] * 2
        + [compact_v] * 2
        + [vmem(kappa.shape), vmem(table_t.shape, jnp.int32)]
        + layers_v
        + weight_rows
        + [smem, dma(7)],
        "inner",
        52,
        10**10,
        out_specs=[spec_hbm()] * 4,
    )(lewis, xlo, grid, kappa, table, offset, *layers)

    zmat = jnp.asarray(tab["zmat"])
    halos = (yprev, ynext, xprev, xnext)
    pad_v = vmem((PADW, PADW, kinds, depth))
    wave, p2, rates = call(
        functools.partial(outer_kernel, **sizes),
        [sds((devices * keep, LANES), f32), sds(cells4, f32), compacted],
        [spec_smem()] * 3
        + [spec_vmem()] * 4
        + [spec_hbm()] * 15,
        [pad_v, pad_v, vmem(cells4), compact_v, compact_v, vmem(kappa.shape), vmem(vel.shape)]
        + [vmem(table_t.shape, jnp.int32), vmem(place_t.shape, jnp.int32)]
        + [vmem(v.shape, v.dtype) for v in (zmat,)]
        + layers_v
        + weight_rows
        + [vmem((slots + 8, LANES)), vmem((rows, depth)), smem, dma(13), dma(8)],
        "outer",
        52,
        10**10,
        out_specs=[spec_vmem(), spec_hbm(), spec_hbm()],
    )(
        count,
        release,
        lewis,
        *halos,
        zmat,
        grid.reshape(cells4),
        p1.reshape(cells4),
        p2.reshape(cells4),
        compact,
        rates,
        kappa,
        vel,
        table,
        place,
        offset,
        *layers,
    )

    wave = lax.all_to_all(wave, ("gx", "gy"), 0, 0, tiled=True)
    consts = tuple(jnp.asarray(tab[k]) for k in ("qy", "qyt", "bx", "bxt", "pick", "kind", "inv"))
    species_out, qy, qyt, bx, bxt, pick, kind, inv = call(
        functools.partial(species_kernel, **sizes),
        [same(sp3)] + [same(v) for v in consts],
        [spec_hbm()] * 11,
        [lines_v, compact_v, vmem(place_t.shape, jnp.int32), smem, padded_species]
        + [dma(10), dma(4), dma(4)],
        "species",
        52,
        5 * 10**9,
        out_specs=[spec_hbm()] + [spec_vmem()] * 7,
    )(*consts, p2.reshape(lines_t.shape), rates, place, offset)

    me = lax.axis_index("gx") * nb + lax.axis_index("gy")
    lam_here = lax.dynamic_slice(jnp.asarray(tab["lamz"]), (me * modes,), (modes,))
    lam = tab["lamx"] + jnp.tile(lam_here, wx * na)[:, None]
    plane_rows = wx * na * modes
    back = pl.pallas_call(
        functools.partial(solve_kernel, na=na, nb=nb, wide=wy, keep=keep),
        out_shape=sds((devices * (keep + 1), LANES), f32),
        in_specs=[spec_vmem()] * 9,
        out_specs=spec_vmem(),
        scratch_shapes=[
            pltpu.VMEM((plane_rows, wy * nb), f32),
            pltpu.VMEM((devices * keep, LANES), f32),
        ],
        compiler_params=params(12),
        name="solve",
    )(
        wave,
        lam,
        tab["lamy"],
        qy,
        qyt,
        bx,
        bxt,
        pick,
        kind,
    )

    back = lax.all_to_all(back, ("gx", "gy"), 0, 0, tiled=True)

    velocity_out = pl.pallas_call(
        functools.partial(slope_kernel, wx=wx, wy=wy, modes=modes),
        out_shape=sds((3 * rows, depth), f32),
        in_specs=[spec_vmem()] * 3,
        out_specs=spec_vmem(),
        scratch_shapes=[
            pltpu.VMEM((tab["inv"].shape[0], LANES), f32),
            pltpu.VMEM((modes, LANES, depth), f32),
            pltpu.VMEM((rows + wy, depth), f32),
        ],
        compiler_params=params(12),
        name="slope",
    )(back, inv, vel)
    return (species_out.reshape(species.shape), velocity_out.reshape(velocity.shape))


def solution(mesh):
    return jax.shard_map(
        per_device,
        mesh=mesh,
        in_specs=(
            P(None, "gx", "gy", None),
            P("gx", "gy", None),
            P(),
            P(None, "gx", "gy", None),
            P(),
            P(),
            P(),
            P(),
            P(),
            P("gx", "gy", None),
            P("gx", "gy"),
        ),
        out_specs=(P(None, "gx", "gy", None), P(None, "gx", "gy", None)),
        check_vma=False,
    )
```

```python
import functools

import jax
import jax.numpy as jnp
import numpy as np
from jax import lax
from jax.experimental import pallas as pl
from jax.experimental.pallas import tpu as pltpu
from jax.sharding import PartitionSpec as P

SUBSTEPS = 2
LANES = 128
diffuse_step = 0.03
react_step = 0.5

f32 = jnp.float32
bf16 = jnp.bfloat16
HIGHEST = lax.Precision.HIGHEST
GAP = 8
BATCH = 8
PADW = 20
PADK = 24
TILE = 512


def dot(a, b, precision=None):
    return jnp.dot(a, b, preferred_element_type=f32, precision=precision)


def dot_nt(a, b):
    return lax.dot_general(a, b, (((1,), (1,)), ((), ())), preferred_element_type=f32)


def spec_vmem():
    return pl.BlockSpec(memory_space=pltpu.VMEM)


def spec_smem():
    return pl.BlockSpec(memory_space=pltpu.SMEM)


def silu(value):
    half = 0.5 * value
    return half * jnp.tanh(half) + half


def spec_any():
    return pl.BlockSpec(memory_space=pl.ANY)


def spec_hbm():
    return pl.BlockSpec(memory_space=pltpu.HBM)


def start_all(pairs, sems):
    copies = [pltpu.make_async_copy(a, b, sems.at[k]) for k, (a, b) in enumerate(pairs)]
    for copy in copies:
        copy.start()
    return copies


def wait_all(copies):
    for copy in copies:
        copy.wait()


def split(value):
    high = value.astype(bf16)
    low = (value - high.astype(f32)).astype(bf16)
    return high, low


def load_species(sp_hbm, sp_pad, rows):
    return [(sp_hbm, sp_pad.at[:, pl.ds(0, rows)])]


def as_lines(ref):
    return ref.reshape(ref.shape[0] * ref.shape[1], *ref.shape[2:])


def y_message_kernel(
    sp_hbm, kappa_hbm, vel_hbm, ylo_ref, yhi_ref, sp_pad, kappa_ref, vel_ref, sems, *, wx, wy, kinds
):
    rows = wx * wy
    pair = 2 * kinds
    step = rows + GAP
    pairs = load_species(sp_hbm, sp_pad, rows)
    sp_ref = as_lines(sp_pad)
    wait_all(start_all([(kappa_hbm, kappa_ref), (vel_hbm, vel_ref)] + pairs, sems))
    for ref, first in ((ylo_ref, 0), (yhi_ref, wy - 2)):
        for x in range(wx):
            ref[pl.ds(x * pair, pair), :] = jnp.concatenate(
                [sp_ref[pl.ds(x * wy + first + k, kinds, stride=step), :] for k in range(2)],
                axis=0,
            ).astype(bf16)
        base = wx * pair
        for k in range(2):
            high, low = split(kappa_ref[pl.ds(first + k, wx, stride=wy), :])
            ref[pl.ds(base + k * wx, wx), :] = high
            ref[pl.ds(base + (2 + k) * wx, wx), :] = low
        high, low = split(vel_ref[pl.ds(rows + first, wx, stride=wy), :])
        ref[pl.ds(base + 4 * wx, wx), :] = high
        ref[pl.ds(base + 5 * wx, wx), :] = low


def own_planes(sp_ref, kappa_ref, vel_ref, grid_ref, xlo_ref, xhi_ref, wx, wy, kinds):
    rows = wx * wy
    pair = 2 * kinds

    @pl.loop(0, wx)
    def _(x):
        for start in range(0, wy, BATCH):
            ys = range(start, start + BATCH)
            lines = [sp_ref[pl.ds(x * wy + y, kinds, stride=rows + GAP), :] for y in ys]
            for y, line in zip(ys, lines):
                grid_ref[x * wy + y] = line

    def cell(x, y):
        return grid_ref[x * wy + y]

    for ref, planes in ((xlo_ref, (0, 1)), (xhi_ref, (wx - 1, wx - 2))):
        for k, x in enumerate(planes):
            for y in range(0, wy, 2):
                ref[pl.ds(k * wy * kinds + y * kinds, pair), :] = jnp.concatenate(
                    [cell(x, y), cell(x, y + 1)], axis=0
                ).astype(bf16)
        base = 2 * wy * kinds
        for k, x in enumerate(planes):
            high, low = split(kappa_ref[pl.ds(x * wy, wy), :])
            ref[pl.ds(base + k * wy, wy), :] = high
            ref[pl.ds(base + (2 + k) * wy, wy), :] = low
        high, low = split(vel_ref[pl.ds(planes[0] * wy, wy), :])
        ref[pl.ds(base + 4 * wy, wy), :] = high
        ref[pl.ds(base + 5 * wy, wy), :] = low


def prepare_kernel(
    count_ref,
    index_hbm,
    before_hbm,
    beforet_hbm,
    upper_hbm,
    sp_hbm,
    kappa_hbm,
    vel_hbm,
    grid_ref,
    xlo_ref,
    xhi_ref,
    table_hbm,
    place_hbm,
    offset_hbm,
    table_ref,
    place_ref,
    offset_ref,
    sp_pad,
    kappa_ref,
    vel_ref,
    index_ref,
    before_ref,
    beforet_ref,
    upper_ref,
    onerow,
    onecol,
    sems,
    *,
    wx,
    wy,
    kinds,
):
    copies = start_all(
        [
            (index_hbm, index_ref),
            (before_hbm, before_ref),
            (beforet_hbm, beforet_ref),
            (upper_hbm, upper_ref),
            (kappa_hbm, kappa_ref),
            (vel_hbm, vel_ref),
        ]
        + load_species(sp_hbm, sp_pad, wx * wy),
        sems,
    )
    wait_all(copies[:4])
    list_kernel(
        count_ref,
        index_ref,
        before_ref,
        beforet_ref,
        upper_ref,
        table_ref,
        place_ref,
        offset_ref,
        onerow,
        onecol,
        rows=wx * wy,
    )
    wait_all(copies[4:])
    outs = start_all(
        [(offset_ref, offset_hbm), (table_ref, table_hbm), (place_ref, place_hbm)], sems
    )
    own_planes(as_lines(sp_pad), kappa_ref, vel_ref, grid_ref, xlo_ref, xhi_ref, wx, wy, kinds)
    wait_all(outs)


def x_message_kernel(yprev, ynext, ownlo_ref, ownhi_ref, xlo_ref, xhi_ref, *, wx, wy, kinds):
    own = ownlo_ref.shape[0]
    pair = 2 * kinds
    ybase = wx * pair
    xlo_ref[pl.ds(0, own), :] = ownlo_ref[...]
    xhi_ref[pl.ds(0, own), :] = ownhi_ref[...]
    for ref, x in ((xlo_ref, 0), (xhi_ref, wx - 1)):
        at = own
        for halo, k in ((yprev, 1), (ynext, 0)):
            ref[pl.ds(at, pair), :] = halo[pl.ds(x * pair, pair), :]
            at += pair
            for part in (k, 2 + k):
                ref[pl.ds(at, wx), :] = halo[pl.ds(ybase + part * wx, wx), :]
                at += wx


def list_kernel(count_ref, index_ref, before_ref, beforet_ref, upper_ref, table_ref, place_ref, offset_ref, onerow, onecol, *, rows):
    count = count_ref[0]
    capacity = index_ref.shape[1]
    step = 512
    parts = capacity // step

    def parts_of(j):
        number = index_ref[:, pl.ds(j * step, step)]
        valid = (lax.broadcasted_iota(jnp.int32, (1, step), 1) + j * step) < count
        row = jnp.where(valid, number // LANES, -1)
        return row, number % LANES, valid

    mask = jnp.zeros((rows, LANES), f32)
    for j in range(parts):
        row, col, valid = parts_of(j)
        hit = lax.broadcasted_iota(jnp.int32, (rows, step), 0) == row
        onerow[:, j * step : (j + 1) * step] = hit.astype(f32).astype(bf16)
        hit = lax.broadcasted_iota(jnp.int32, (LANES, step), 0) == col
        onecol[:, j * step : (j + 1) * step] = hit.astype(f32).astype(bf16)
    mask = dot_nt(onerow[...], onecol[...])
    maskb = mask.astype(bf16)
    rank = dot(maskb, upper_ref[...])
    total = dot(maskb, jnp.ones((LANES, LANES), bf16))
    offset = dot(before_ref[...], total.astype(bf16))
    total_row = dot_nt(jnp.ones((8, LANES), bf16), maskb)
    offset_ref[...] = dot(total_row.astype(bf16), beforet_ref[...]).astype(jnp.int32)
    place = (offset + rank).astype(jnp.int32)
    place_hi = (place // LANES).astype(f32)
    place_lo = (place % LANES).astype(f32)
    place_ref[...] = jnp.where(mask > 0.5, place % LANES, place % LANES - LANES)
    both = jnp.concatenate([place_hi.T, place_lo.T], axis=0).astype(bf16)
    table = jnp.zeros(table_ref.shape, f32)
    for j in range(parts):
        row, col, valid = parts_of(j)
        found = dot(both, onerow[:, j * step : (j + 1) * step])
        colf = onecol[:, j * step : (j + 1) * step].astype(f32)
        hi = jnp.sum(found[:LANES] * colf, axis=0, keepdims=True)
        lo = jnp.sum(found[LANES:] * colf, axis=0, keepdims=True)
        hi = jnp.where(valid, hi, -1.0).astype(jnp.int32)
        lo = lo.astype(jnp.int32)
        put_hi = jnp.where(
            lax.broadcasted_iota(jnp.int32, (table_ref.shape[0], step), 0) == hi,
            col.astype(f32),
            0.0,
        ).astype(bf16)
        put_lo = (
            (lax.broadcasted_iota(jnp.int32, (LANES, step), 0) == lo).astype(f32).astype(bf16)
        )
        table = table + dot_nt(put_hi, put_lo)
    table_ref[...] = table.astype(jnp.int32)


def make_weights(kp, we, wn, wu, wd, ws, wx):
    scale = 0.5 * diffuse_step

    def line(px):
        base = px * PADK
        here = kp[pl.ds(base, PADK), :]
        up = jnp.roll(here, -1, 1)
        wu_v = scale * (here + up)
        we_v = scale * (here + kp[pl.ds(base + PADK, PADK), :])
        wn_v = scale * (here + kp[pl.ds(base + 1, PADK), :])
        ww_v = scale * (here + kp[pl.ds(base - PADK, PADK), :])
        wsouth = scale * (here + kp[pl.ds(base - 1, PADK), :])
        wd_v = jnp.roll(wu_v, 1, 1)
        we[pl.ds(base, PADK), :] = we_v
        wn[pl.ds(base, PADK), :] = wn_v
        wu[pl.ds(base, PADK), :] = wu_v
        wd[pl.ds(base, PADK), :] = wd_v
        ws[pl.ds(base, PADK), :] = ((we_v + ww_v) + (wn_v + wsouth)) + (wu_v + wd_v)

    for px in range(1, wx + 3):
        line(px)
    base = 0
    here = kp[pl.ds(base, PADK), :]
    we[pl.ds(base, PADK), :] = scale * (here + kp[pl.ds(base + PADK, PADK), :])


def cell_update(src, row, line, px, py, weights, lewis):
    we, wn, wu, wd, ws = weights
    kr = px * PADK + py

    def w(ref, r):
        return ref[pl.ds(r, 1), :]

    here = src[row]
    total = w(we, kr) * src[row + line] + w(we, kr - PADK) * src[row - line]
    total = total + (w(wn, kr) * src[row + 1] + w(wn, kr - 1) * src[row - 1])
    total = total + (w(wu, kr) * jnp.roll(here, -1, 1) + w(wd, kr) * jnp.roll(here, 1, 1))
    total = total - w(ws, kr) * here
    return here + lewis * total


def pad_row(px, py):
    return px * PADW + py


def update_cells(src, dst, cells, src_row, dst_row, line, weights, lewis):
    for start in range(0, len(cells), 4):
        part = cells[start : start + 4]
        values = [cell_update(src, src_row(px, py), line, px, py, weights, lewis) for px, py in part]
        for (px, py), value in zip(part, values):
            dst[dst_row(px, py)] = value


def column(scalars, kinds):
    row = lax.broadcasted_iota(jnp.int32, (kinds, LANES), 0)
    value = jnp.full((kinds, LANES), scalars[0], f32)
    for s in range(1, kinds):
        value = jnp.where(row == s, scalars[s], value)
    return value


def fill_own(kp, kappa_ref, wx, wy):
    for x in range(wx):
        kp[pl.ds((x + 2) * PADK + 2, wy), :] = kappa_ref[pl.ds(x * wy, wy), :]


def collect(listed, p2, table_ref, offset_s, compact, kinds):
    lane = lax.broadcasted_iota(jnp.int32, (1, LANES), 1)
    for start in range(0, len(listed), BATCH):
        ready = []
        for r in listed[start : start + BATCH]:
            offset = offset_s[0, r]
            hi = offset // LANES
            later = lane >= offset % LANES
            pick = jnp.where(later, table_ref[pl.ds(hi, 1), :], table_ref[pl.ds(hi + 1, 1), :])
            got = jnp.take_along_axis(
                p2[r], jnp.broadcast_to(pick, (kinds, LANES)), axis=1, mode="promise_in_bounds"
            )
            ready.append((hi, later, got))
        for hi, later, got in ready:
            pltpu.store(compact.at[hi], got, mask=jnp.broadcast_to(later, (kinds, LANES)))
            compact[hi + 1] = got


def spread(r, rates, place_ref, offset_s, kinds):
    lane = lax.broadcasted_iota(jnp.int32, (1, LANES), 1)
    offset = offset_s[0, r]
    hi = offset // LANES
    lo = offset % LANES
    merged = jnp.where(jnp.broadcast_to(lane >= lo, (kinds, LANES)), rates[hi], rates[hi + 1])
    place = place_ref[pl.ds(r, 1), :]
    live = jnp.broadcast_to(place >= 0, (kinds, LANES))
    pick = jnp.broadcast_to(place & (LANES - 1), (kinds, LANES))
    got = jnp.take_along_axis(merged, pick, axis=1, mode="promise_in_bounds")
    return jnp.where(live, got, 0.0)


def network_tile(t, compact, rates, w1_ref, w2_ref, w3_ref, w4_ref):
    blocks = TILE // LANES
    cells = jnp.concatenate([compact[t * blocks + k] for k in range(blocks)], axis=1)
    hidden = silu(dot(w1_ref[...], cells.astype(bf16))).astype(bf16)
    hidden = silu(dot(w2_ref[...], hidden)).astype(bf16)
    hidden = silu(dot(w3_ref[...], hidden)).astype(bf16)
    result = dot(w4_ref[...], hidden).astype(bf16).astype(f32)
    for k in range(blocks):
        rates[t * blocks + k] = result[:, k * LANES : (k + 1) * LANES]


def inner_kernel(
    lewis_s,
    after_ref,
    p0,
    kappa_hbm,
    table_hbm,
    offset_hbm,
    w1_hbm,
    w2_hbm,
    w3_hbm,
    w4_hbm,
    p1_hbm,
    lines_hbm,
    p1,
    p2,
    compact,
    rates,
    kappa_ref,
    table_ref,
    w1_ref,
    w2_ref,
    w3_ref,
    w4_ref,
    kp,
    we,
    wn,
    wu,
    wd,
    ws,
    offset_s,
    sems,
    *,
    wx,
    wy,
    kinds,
):
    copies = start_all(
        [
            (kappa_hbm, kappa_ref),
            (offset_hbm, offset_s),
            (table_hbm, table_ref),
            (w1_hbm, w1_ref),
            (w2_hbm, w2_ref),
            (w3_hbm, w3_ref),
            (w4_hbm, w4_ref),
        ],
        sems,
    )
    weights = (we, wn, wu, wd, ws)
    lewis = 1.0 / column(lewis_s, kinds)
    copies[0].wait()
    fill_own(kp, kappa_ref, wx, wy)
    make_weights(kp, we, wn, wu, wd, ws, wx)

    def row_of(px, py):
        return (px - 2) * wy + py - 2

    @pl.loop(3, wx + 1)
    def _(px):
        cells = [(px, py) for py in range(3, wy + 1)]
        update_cells(p0, p1, cells, row_of, row_of, wy, weights, lewis)

    @pl.loop(4, wx)
    def _(px):
        cells = [(px, py) for py in range(4, wy)]
        update_cells(p1, p2, cells, row_of, row_of, wy, weights, lewis)

    wait_all(copies[1:])

    @pl.loop(2, wx - 2)
    def _(x):
        listed = [x * wy + y for y in range(2, wy - 2)]
        collect(listed, p2, table_ref, offset_s, compact, kinds)

    rows = wx * wy
    slots = compact.shape[0]
    outs = start_all(
        [
            (p1, p1_hbm),
            (p2, lines_hbm.at[pl.ds(0, rows)]),
            (compact, lines_hbm.at[pl.ds(rows, slots)]),
        ],
        sems,
    )

    @pl.loop(0, offset_s[0, 0] // TILE)
    def _(t):
        network_tile(t, compact, rates, w1_ref, w2_ref, w3_ref, w4_ref)

    wait_all(outs)
    wait_all(start_all([(rates, lines_hbm.at[pl.ds(rows + slots, slots)])], sems))


def ring_copies(src, dst, wx, wy, inset):
    pairs = []
    wide_x = (inset, wx - 2 * inset)
    wide_y = (inset, wy - 2 * inset)
    for xs, ys in (
        ((inset, 2), wide_y),
        ((wx - inset - 2, 2), wide_y),
        (wide_x, (inset, 2)),
        (wide_x, (wy - inset - 2, 2)),
    ):
        if ys[1] == 2:
            xs = (xs[0] + 2, xs[1] - 4)
        pairs.append(
            (
                src.at[pl.ds(*xs), pl.ds(*ys)],
                dst.at[pl.ds(xs[0] + 2, xs[1]), pl.ds(ys[0] + 2, ys[1])],
            )
        )
    return pairs


def outer_kernel(
    count_ref,
    heat_s,
    lewis_s,
    yprev_ref,
    ynext_ref,
    xprev_ref,
    xnext_ref,
    zmat_hbm,
    grid_hbm,
    p1_hbm,
    inner_hbm,
    lines_hbm,
    kappa_hbm,
    vel_hbm,
    table_hbm,
    place_hbm,
    offset_hbm,
    w1_hbm,
    w2_hbm,
    w3_hbm,
    w4_hbm,
    out_ref,
    lines_out,
    pad0,
    pad1,
    slab2,
    compact,
    rates,
    kappa_ref,
    vel_ref,
    table_ref,
    place_ref,
    zmat_ref,
    w1_ref,
    w2_ref,
    w3_ref,
    w4_ref,
    kp,
    we,
    wn,
    wu,
    wd,
    ws,
    heat_slots,
    heat_rows,
    offset_s,
    sems,
    ring_sems,
    *,
    wx,
    wy,
    kinds,
):
    rows = wx * wy
    slots = compact.shape[0]
    rings = start_all(
        ring_copies(grid_hbm, pad0, wx, wy, 0) + ring_copies(p1_hbm, pad1, wx, wy, 1), ring_sems
    )
    p0 = as_lines(pad0)
    p1 = as_lines(pad1)
    p2 = as_lines(slab2)
    mid = (pl.ds(2, wx - 4), pl.ds(2, wy - 4))
    copies = start_all(
        [
            (kappa_hbm, kappa_ref),
            (offset_hbm, offset_s),
            (table_hbm, table_ref),
            (lines_hbm.at[pl.ds(rows, slots)], compact),
            (lines_hbm.at[pl.ds(rows + slots, slots)], rates),
            (w1_hbm, w1_ref),
            (w2_hbm, w2_ref),
            (w3_hbm, w3_ref),
            (w4_hbm, w4_ref),
            (place_hbm, place_ref),
            (vel_hbm, vel_ref),
            (zmat_hbm, zmat_ref),
            (inner_hbm.at[mid], slab2.at[mid]),
        ],
        sems,
    )
    pair = 2 * kinds
    weights = (we, wn, wu, wd, ws)
    lewis = 1.0 / column(lewis_s, kinds)
    wait_all(copies[:1])
    fill_own(kp, kappa_ref, wx, wy)
    ybase = wx * pair
    for ref, py in ((yprev_ref, 0), (ynext_ref, wy + 2)):
        for x in range(wx):
            both = ref[pl.ds(x * pair, pair), :].astype(f32)
            p0[(x + 2) * PADW + py] = both[:kinds]
            p0[(x + 2) * PADW + py + 1] = both[kinds:]
        for k in range(2):
            value = ref[pl.ds(ybase + k * wx, wx), :].astype(f32) + ref[
                pl.ds(ybase + (2 + k) * wx, wx), :
            ].astype(f32)
            kp[pl.ds(2 * PADK + py + k, wx, stride=PADK), :] = value
    xbase = 2 * wy * kinds
    cbase = xbase + 6 * wy
    for ref, near, far, edge in ((xprev_ref, 1, 0, wx - 1), (xnext_ref, wx + 2, wx + 3, 0)):
        for k, px in ((0, near), (1, far)):
            for y in range(0, wy, 2):
                both = ref[pl.ds(k * wy * kinds + y * kinds, pair), :].astype(f32)
                p0[px * PADW + y + 2] = both[:kinds]
                p0[px * PADW + y + 3] = both[kinds:]
            value = ref[pl.ds(xbase + k * wy, wy), :].astype(f32) + ref[
                pl.ds(xbase + (2 + k) * wy, wy), :
            ].astype(f32)
            kp[pl.ds(px * PADK + 2, wy), :] = value
        piece = pair + 2 * wx
        for k, py in ((0, 1), (1, wy + 2)):
            start = cbase + k * piece
            both = ref[pl.ds(start, pair), :].astype(f32)
            p0[near * PADW + py] = both[kinds:] if k == 0 else both[:kinds]
            value = ref[pl.ds(start + pair, wx), :].astype(f32) + ref[
                pl.ds(start + pair + wx, wx), :
            ].astype(f32)
            kp[pl.ds(near * PADK + py, 1), :] = value[edge : edge + 1]
    make_weights(kp, we, wn, wu, wd, ws, wx)

    def second_row(px, py):
        return (px - 2) * wy + py - 2

    wait_all(rings)

    def first(cells):
        update_cells(p0, p1, cells, pad_row, pad_row, PADW, weights, lewis)

    def second(cells):
        update_cells(p1, p2, cells, pad_row, second_row, PADW, weights, lewis)

    @pl.loop(0, 2)
    def _(k):
        first([(1 + k * (wx + 1), py) for py in range(2, wy + 2)])
        first([(2 + k * (wx - 1), py) for py in range(1, wy + 3)])

    @pl.loop(3, wx + 1)
    def _(px):
        first([(px, py) for py in (1, 2, wy + 1, wy + 2)])

    @pl.loop(0, 2)
    def _(k):
        second([(2 + k * (wx - 2), py) for py in range(2, wy + 2)])
        second([(3 + k * (wx - 2), py) for py in range(2, wy + 2)])

    @pl.loop(4, wx)
    def _(px):
        second([(px, py) for py in (2, 3, wy, wy + 1)])

    wait_all(copies[1:])
    outs = start_all([(p2, lines_out.at[pl.ds(0, rows)])], ring_sems)

    def take(listed):
        collect(listed, p2, table_ref, offset_s, compact, kinds)

    @pl.loop(0, 2)
    def _(x):
        take([x * wy + y for y in range(wy)])

    @pl.loop(0, (wx - 4) // 2)
    def _(k):
        edge = (0, 1, wy - 2, wy - 1)
        take([(2 + 2 * k + i) * wy + y for i in range(2) for y in edge])

    @pl.loop(wx - 2, wx)
    def _(x):
        take([x * wy + y for y in range(wy)])

    count = count_ref[0]

    @pl.loop(offset_s[0, 0] // TILE, (count + TILE - 1) // TILE)
    def _(t):
        network_tile(t, compact, rates, w1_ref, w2_ref, w3_ref, w4_ref)

    wait_all(outs)
    outs = start_all([(rates, lines_out.at[pl.ds(rows, slots)])], ring_sems)
    release = column(heat_s, kinds)
    for k in range(heat_slots.shape[0] // BATCH):
        heat_slots[pl.ds(k * BATCH, BATCH), :] = jnp.concatenate(
            [
                jnp.sum(release * rates[k * BATCH + i], axis=0, keepdims=True)
                for i in range(BATCH)
            ],
            axis=0,
        )
    lane = lax.broadcasted_iota(jnp.int32, (1, LANES), 1)

    @pl.loop(0, rows // BATCH)
    def _(k):
        lines = []
        for i in range(BATCH):
            offset = offset_s[0, k * BATCH + i]
            hi = offset // LANES
            later = lane >= offset % LANES
            lines.append(
                jnp.where(later, heat_slots[pl.ds(hi, 1), :], heat_slots[pl.ds(hi + 1, 1), :])
            )
        at = pl.ds(pl.multiple_of(k * BATCH, BATCH), BATCH)
        place = place_ref[at, :]
        got = jnp.take_along_axis(
            jnp.concatenate(lines, axis=0),
            place & (LANES - 1),
            axis=1,
            mode="promise_in_bounds",
        )
        heat_rows[at, :] = jnp.where(place >= 0, got, 0.0)

    ux = vel_ref[pl.ds(0, rows), :]
    nextx = xnext_ref[pl.ds(xbase + 4 * wy, wy), :].astype(f32) + xnext_ref[
        pl.ds(xbase + 5 * wy, wy), :
    ].astype(f32)
    east = jnp.concatenate([ux[wy:], nextx], axis=0)
    nexty = ynext_ref[pl.ds(ybase + 4 * wx, wx), :].astype(f32) + ynext_ref[
        pl.ds(ybase + 5 * wx, wx), :
    ].astype(f32)
    uy = vel_ref[pl.ds(rows, rows), :]
    north = vel_ref[pl.ds(rows + 1, rows), :]
    last = lax.broadcasted_iota(jnp.int32, (wy, LANES), 0) == wy - 1
    pieces = []
    for x in range(wx):
        pieces.append(
            jnp.where(
                last,
                jnp.broadcast_to(nexty[x : x + 1], (wy, LANES)),
                north[x * wy : (x + 1) * wy],
            )
        )
    north = jnp.concatenate(pieces, axis=0)
    uz = vel_ref[pl.ds(2 * rows, rows), :]
    source = (east - ux) + (north - uy) + (jnp.roll(uz, -1, 1) - uz) - heat_rows[...]
    turned = jnp.concatenate(
        [source[h * LANES : (h + 1) * LANES].T for h in range(rows // LANES)], axis=0
    )
    out_ref[...] = dot(zmat_ref[...], turned, HIGHEST)
    wait_all(outs)


def early_lines(wx, wy):
    return wx * 3 // 8 * wy


def species_lines(start, count, p2_hbm, spec_hbm, p2, rates, place_ref, offset_s, stage, first, in_sems, out_sems, kinds, rows):
    parts = in_sems.shape[0]
    size = count // parts
    chunks = [pl.ds(start + c * size, size) for c in range(parts)]
    loads = start_all([(p2_hbm.at[c], p2.at[c]) for c in chunks], in_sems)
    lines_out = as_lines(stage)
    wait_all(first)
    stores = []
    for c in range(parts):
        loads[c].wait()
        begin = (start + c * size) // BATCH

        @pl.loop(begin, begin + size // BATCH)
        def _(k):
            lines = []
            for i in range(BATCH):
                r = k * BATCH + i
                lines.append(p2[r] + react_step * spread(r, rates, place_ref, offset_s, kinds))
            for i in range(BATCH):
                lines_out[pl.ds(k * BATCH + i, kinds, stride=rows + GAP), :] = lines[i]

        copy = pltpu.make_async_copy(
            stage.at[:, chunks[c]], spec_hbm.at[:, chunks[c]], out_sems.at[c]
        )
        copy.start()
        stores.append(copy)
    wait_all(stores)


def species_kernel(
    qy_hbm,
    qyt_hbm,
    bx_hbm,
    bxt_hbm,
    pick_hbm,
    kind_hbm,
    p2_hbm,
    place_hbm,
    offset_hbm,
    spec_hbm,
    qy_ref,
    qyt_ref,
    bx_ref,
    bxt_ref,
    pick_ref,
    kind_ref,
    p2,
    rates,
    place_ref,
    offset_s,
    stage,
    sems,
    in_sems,
    out_sems,
    *,
    wx,
    wy,
    kinds,
):
    rows = wx * wy
    copies = start_all(
        [
            (offset_hbm, offset_s),
            (place_hbm, place_ref),
            (p2_hbm.at[pl.ds(wx * wy, rates.shape[0])], rates),
            (qy_hbm, qy_ref),
            (qyt_hbm, qyt_ref),
            (bx_hbm, bx_ref),
            (bxt_hbm, bxt_ref),
            (pick_hbm, pick_ref),
            (kind_hbm, kind_ref),
        ],
        sems,
    )
    species_lines(0, early_lines(wx, wy), p2_hbm, spec_hbm, p2, rates, place_ref, offset_s, stage, copies[:3], in_sems, out_sems, kinds, rows)
    wait_all(copies[3:])


def species_rest_kernel(
    after_ref,
    spec_in,
    inv_hbm,
    p2_hbm,
    place_hbm,
    offset_hbm,
    spec_hbm,
    inv_ref,
    p2,
    rates,
    place_ref,
    offset_s,
    stage,
    sems,
    in_sems,
    out_sems,
    *,
    wx,
    wy,
    kinds,
):
    first = start_all([(inv_hbm, inv_ref), (offset_hbm, offset_s), (place_hbm, place_ref), (p2_hbm.at[pl.ds(wx * wy, rates.shape[0])], rates)], sems)
    early = early_lines(wx, wy)
    species_lines(early, wx * wy - early, p2_hbm, spec_hbm, p2, rates, place_ref, offset_s, stage, first, in_sems, out_sems, kinds, wx * wy)


def solve_kernel(
    in_ref, lam_ref, lamy_ref, qy_ref, qyt_ref, bx_ref, bxt_ref, pick_ref, kind_ref, out_ref, lines, tiles, *, na, nb, wide, keep
):
    groups = LANES // wide
    spans = nb // groups
    lane = lax.broadcasted_iota(jnp.int32, (1, LANES), 1) // wide
    for a in range(na):
        for span in range(spans):
            blocks = [
                in_ref[pl.ds((a * nb + span * groups + g) * keep, keep), :] for g in range(groups)
            ]
            for g in range(groups):
                line = blocks[g]
                for b in range(groups):
                    if b != g:
                        moved = pltpu.roll(blocks[b], ((b - g) * wide) % LANES, 1)
                        line = jnp.where(lane == b, moved, line)
                lines[pl.ds((g * na + a) * keep, keep), span * LANES : (span + 1) * LANES] = line
    wave = dot(bx_ref[...], dot(lines[...], qyt_ref[...], HIGHEST), HIGHEST)
    lam = lam_ref[...] + lamy_ref[...]
    anchor = lam == 0.0
    wave = jnp.where(anchor, 0.0, wave / jnp.where(anchor, 1.0, lam))
    lines[...] = dot(dot(bxt_ref[...], wave, HIGHEST), qy_ref[...], HIGHEST)
    for a in range(na):
        for span in range(spans):
            blocks = [
                lines[pl.ds((g * na + a) * keep, keep), span * LANES : (span + 1) * LANES]
                for g in range(groups)
            ]
            for b in range(groups):
                tile = blocks[b]
                for g in range(groups):
                    if b != g:
                        moved = pltpu.roll(blocks[g], ((g - b) * wide) % LANES, 1)
                        tile = jnp.where(lane == g, moved, tile)
                where = a * nb + span * groups + b
                tiles[pl.ds(where * keep, keep), :] = tile
                for k in range(keep):
                    out_ref[pl.ds(where, 1), k * LANES : (k + 1) * LANES] = tile[k : k + 1]
    south_pick = pick_ref[pl.ds(0, keep), :]
    west_pick = pick_ref[pl.ds(keep, keep), :]
    kind = kind_ref[...]
    for a in range(na):
        for b in range(nb):
            south = tiles[pl.ds((a * nb + (b - 1) % nb) * keep, keep), :]
            west = tiles[pl.ds(((a - 1) % na * nb + b) * keep, keep), :]
            south = jnp.take_along_axis(south, south_pick, axis=1, mode="promise_in_bounds")
            west = jnp.take_along_axis(west, west_pick, axis=1, mode="promise_in_bounds")
            both = jnp.where(kind == 1, south, jnp.where(kind == 2, west, 0.0))
            out_ref[pl.ds(a * nb + b, 1), keep * LANES :] = jnp.sum(both, axis=0, keepdims=True)


def slope_kernel(in_ref, inv_ref, vel_ref, out_ref, padded, extra, field, *, wx, wy, modes):
    rows = wx * wy
    halves = rows // LANES
    devices = in_ref.shape[0]
    total = devices * (in_ref.shape[1] // LANES)
    full = padded.shape[0]
    for k in range(total // devices):
        padded[pl.ds(k * devices, devices), :] = in_ref[:, k * LANES : (k + 1) * LANES]
    if full > total:
        padded[pl.ds(total, full - total), :] = jnp.zeros((full - total, LANES), f32)
    turned = jnp.concatenate(
        [padded[pl.ds(k * LANES, LANES), :].T for k in range(full // LANES)], axis=1
    )
    wave = dot(turned, inv_ref[...], HIGHEST)
    for h in range(halves):
        field[pl.ds(wy + h * LANES, LANES), :] = wave[:, h * LANES : (h + 1) * LANES]
    for m in range(modes):
        extra[m] = wave[:, (halves + m) * LANES : (halves + m + 1) * LANES]
    south = []
    west = []
    lines = LANES // wy
    for h in range(halves):
        south.append(sum(extra[m, pl.ds(h * modes + m, lines, stride=wy), :] for m in range(modes)))
    for g in range(2):
        west.append(sum(extra[m, pl.ds((m * 2 + g) * wy + wy // 2, wy // 2), :] for m in range(modes)))
    field[pl.ds(0, wy), :] = jnp.concatenate(west, axis=0)
    here = field[pl.ds(wy, rows), :]
    out_ref[pl.ds(0, rows), :] = vel_ref[pl.ds(0, rows), :] - (here - field[pl.ds(0, rows), :])
    first = lax.broadcasted_iota(jnp.int32, (wy, LANES), 0) == 0
    for x in range(wx):
        behind = field[pl.ds(wy - 1 + x * wy, wy), :]
        edge = south[x // lines][x % lines : x % lines + 1]
        behind = jnp.where(first, jnp.broadcast_to(edge, (wy, LANES)), behind)
        at = pl.ds(rows + x * wy, wy)
        out_ref[at, :] = vel_ref[at, :] - (here[x * wy : (x + 1) * wy] - behind)
    at = pl.ds(2 * rows, rows)
    out_ref[at, :] = vel_ref[at, :] - (here - jnp.roll(here, 1, 1))


def real_basis(n):
    at = np.arange(n)
    basis = np.zeros((n, n))
    waves = np.zeros(n, dtype=np.int64)
    basis[0] = 1.0 / np.sqrt(n)
    for k in range(1, (n + 1) // 2):
        angle = 2.0 * np.pi * ((k * at) % n) / n
        basis[2 * k - 1] = np.sqrt(2.0 / n) * np.cos(angle)
        basis[2 * k] = np.sqrt(2.0 / n) * np.sin(angle)
        waves[2 * k - 1] = k
        waves[2 * k] = k
    if n % 2 == 0:
        basis[n - 1] = np.where(at % 2 == 0, 1.0, -1.0) / np.sqrt(n)
        waves[n - 1] = n // 2
    return basis, -4.0 * np.sin(np.pi * waves / n) ** 2


@functools.lru_cache(maxsize=None)
def plan(wx, wy, depth, na, nb):
    rows = wx * wy
    halves = rows // LANES
    devices = na * nb
    modes = depth // devices
    keep = halves * modes
    lines = LANES // wy
    zb, lamz = real_basis(depth)
    qx, lamx = real_basis(wx * na)
    qy, lamy = real_basis(wy * nb)
    zmat = np.zeros((devices, halves, modes, halves, depth))
    for h in range(halves):
        zmat[:, h, :, h, :] = zb.reshape(devices, modes, depth)
    zmat = zmat.reshape(devices * keep, halves * depth)
    inv = np.zeros((devices, keep + 1, halves + modes, depth))
    for h in range(halves):
        for m in range(modes):
            inv[:, h * modes + m, h, :] = zb.reshape(devices, modes, depth)[:, m]
    for m in range(modes):
        inv[:, keep, halves + m, :] = zb.reshape(devices, modes, depth)[:, m]
    inv = inv.swapaxes(0, 1).reshape(devices * (keep + 1), (halves + modes) * depth)
    full = -(-inv.shape[0] // LANES) * LANES
    inv = np.pad(inv, ((0, full - inv.shape[0]), (0, 0)))
    bx = np.zeros((wx * na, modes, lines, na, halves, modes))
    for g in range(lines):
        for a in range(na):
            for h in range(halves):
                for m in range(modes):
                    bx[:, m, g, a, h, m] = qx[:, a * wx + h * lines + g]
    bx = bx.reshape(wx * na * modes, lines * na * keep)
    pick = np.zeros((2, keep, LANES), np.int32)
    kind = np.zeros((keep, LANES), np.int32)
    for k in range(keep):
        for g in range(lines):
            pick[0, k, g * wy + k] = g * wy + wy - 1
            kind[k, g * wy + k] = 1
    for m in range(modes):
        for y in range(wy):
            to = (m * 2 + y // (wy // 2)) * wy + wy // 2 + y % (wy // 2)
            pick[1, (halves - 1) * modes + m, to] = LANES - wy + y
            kind[(halves - 1) * modes + m, to] = 2
    inner = [
        x * wy + y for x in range(wx) for y in range(wy) if 2 <= x < wx - 2 and 2 <= y < wy - 2
    ]
    outer = [r for r in range(rows) if r not in set(inner)]
    order = np.array(inner + outer)
    turn = np.empty(rows, np.int64)
    turn[order] = np.arange(rows)
    before = turn[None, :] < turn[:, None]
    upper = np.arange(LANES)[:, None] < np.arange(LANES)[None, :]
    as32 = lambda v: np.asarray(v, np.float32)
    as16 = lambda v: np.asarray(v, np.float32).astype(jnp.bfloat16)
    return dict(
        zmat=as32(zmat),
        inv=as32(inv),
        bx=as32(bx),
        bxt=as32(bx.T),
        qy=as32(qy),
        qyt=as32(qy.T),
        lamx=as32(np.repeat(lamx, modes)[:, None]),
        lamy=as32(lamy[None, :]),
        lamz=as32(lamz),
        pick=pick.reshape(2 * keep, LANES),
        kind=kind,
        order=order.astype(np.int32),
        before=as16(before),
        beforet=as16(before.T),
        upper=as16(upper),
        inner=len(inner),
    )


def shift(value, axis, by):
    peers = lax.axis_size(axis)
    return lax.ppermute(value, axis, [(i, (i + by) % peers) for i in range(peers)])


def params(megabytes):
    return pltpu.CompilerParams(vmem_limit_bytes=megabytes * 2**20)


def per_device(
    species,
    diffusivity,
    lewis_number,
    velocity,
    layer_one,
    layer_two,
    layer_three,
    layer_four,
    heat_release,
    react_index,
    react_count,
):
    kinds, wx, wy, depth = species.shape
    na = lax.axis_size("gx")
    nb = lax.axis_size("gy")
    devices = na * nb
    rows = wx * wy
    halves = rows // LANES
    modes = depth // devices
    keep = halves * modes
    tab = plan(wx, wy, depth, na, nb)
    sp = species.reshape(kinds * rows, depth)
    kappa = diffusivity.reshape(rows, depth)
    vel = velocity.reshape(3 * rows, depth)
    count = react_count.reshape(1)
    capacity = react_index.size
    slots = capacity // LANES
    sds = jax.ShapeDtypeStruct
    own = 2 * wy * kinds + 6 * wy

    def call(body, outs, ins, scratch, name, megabytes, flops, aliases=None, out_specs=None):
        return pl.pallas_call(
            body,
            out_shape=outs,
            in_specs=ins,
            out_specs=out_specs or [spec_vmem()] * len(outs),
            scratch_shapes=scratch,
            input_output_aliases=aliases or {},
            compiler_params=params(megabytes),
            cost_estimate=pl.CostEstimate(flops=flops, bytes_accessed=2**20, transcendentals=0),
            name=name,
        )

    def same(array):
        return sds(array.shape, array.dtype)

    def dma(n):
        return pltpu.SemaphoreType.DMA((n,))

    sizes = dict(wx=wx, wy=wy, kinds=kinds)
    def vmem(shape, dtype=f32):
        return pltpu.VMEM(shape, dtype)

    message = sds((own, depth), bf16)
    padded_species = vmem((kinds, rows + GAP, depth))
    sp3 = sp.reshape(kinds, rows, depth)
    own_lines = [padded_species, vmem(kappa.shape), vmem(vel.shape)]
    ylo, yhi = call(
        functools.partial(y_message_kernel, **sizes),
        [message] * 2,
        [spec_hbm()] * 3,
        own_lines + [dma(3)],
        "ymessage",
        52,
        10**7,
    )(sp3, kappa, vel)

    yprev = shift(yhi, "gy", 1)
    ynext = shift(ylo, "gy", -1)

    index = react_index.reshape(1, capacity)
    layers = (layer_one, layer_two, layer_three, layer_four)
    lists = (index, tab["before"], tab["beforet"], tab["upper"])
    table_t = sds((slots + 8, LANES), jnp.int32)
    place_t = sds((rows, LANES), jnp.int32)
    offset_t = sds((8, rows), jnp.int32)
    lines_t = sds((rows, kinds, depth), f32)
    grid, xlo, xhi, table, place, offset = call(
        functools.partial(prepare_kernel, **sizes),
        [lines_t, message, message, table_t, place_t, offset_t],
        [spec_smem()] + [spec_hbm()] * 7,
        [vmem(v.shape, v.dtype) for v in (table_t, place_t, offset_t)]
        + own_lines
        + [vmem(v.shape, v.dtype) for v in lists]
        + [vmem((rows, capacity), bf16), vmem((LANES, capacity), bf16), dma(7)],
        "prepare",
        52,
        5 * 10**9,
        out_specs=[spec_vmem()] * 3 + [spec_hbm()] * 3,
    )(count, *lists, sp3, kappa, vel)

    extra = 2 * (2 * kinds + 2 * wx)
    message = sds((own + extra, depth), bf16)
    xlo, xhi = call(
        functools.partial(x_message_kernel, **sizes),
        [message, message],
        [spec_vmem()] * 4,
        [],
        "xmessage",
        52,
        10**7,
    )(yprev, ynext, xlo, xhi)
    xprev = shift(xhi, "gx", 1)
    xnext = shift(xlo, "gx", -1)

    weight_rows = [vmem((PADW * PADK + 8, depth))] * 6
    layers_v = [vmem(w.shape, w.dtype) for w in layers]
    compacted = sds((slots + 8, kinds, LANES), f32)
    lewis = lewis_number
    release = heat_release
    cells4 = (wx, wy, kinds, depth)
    smem = pltpu.SMEM((8, rows), jnp.int32)
    lines_v = vmem(lines_t.shape)
    compact_v = vmem(compacted.shape)
    passed = rows + 2 * (slots + 8)
    p1, lines = call(
        functools.partial(inner_kernel, **sizes),
        [lines_t, sds((passed, kinds, depth), f32)],
        [spec_smem(), spec_any(), spec_vmem()] + [spec_hbm()] * 7,
        [lines_v] * 2
        + [compact_v] * 2
        + [vmem(kappa.shape), vmem(table_t.shape, jnp.int32)]
        + layers_v
        + weight_rows
        + [smem, dma(7)],
        "inner",
        52,
        10**10,
        out_specs=[spec_hbm()] * 2,
    )(lewis, xlo, grid, kappa, table, offset, *layers)

    zmat = jnp.asarray(tab["zmat"])
    halos = (yprev, ynext, xprev, xnext)
    pad_v = vmem((PADW, PADW, kinds, depth))
    wave, lines = call(
        functools.partial(outer_kernel, **sizes),
        [sds((devices * keep, LANES), f32), sds((rows + slots + 8, kinds, depth), f32)],
        [spec_smem()] * 3
        + [spec_vmem()] * 4
        + [spec_hbm()] * 14,
        [pad_v, pad_v, vmem(cells4), compact_v, compact_v, vmem(kappa.shape), vmem(vel.shape)]
        + [vmem(table_t.shape, jnp.int32), vmem(place_t.shape, jnp.int32)]
        + [vmem(v.shape, v.dtype) for v in (zmat,)]
        + layers_v
        + weight_rows
        + [vmem((slots + 8, LANES)), vmem((rows, depth)), smem, dma(13), dma(8)],
        "outer",
        52,
        10**10,
        out_specs=[spec_vmem(), spec_hbm()],
    )(
        count,
        release,
        lewis,
        *halos,
        zmat,
        grid.reshape(cells4),
        p1.reshape(cells4),
        lines.reshape(passed // wy, wy, kinds, depth),
        lines,
        kappa,
        vel,
        table,
        place,
        offset,
        *layers,
    )

    wave = lax.all_to_all(wave, ("gx", "gy"), 0, 0, tiled=True)
    consts = tuple(jnp.asarray(tab[k]) for k in ("qy", "qyt", "bx", "bxt", "pick", "kind"))
    species_out, qy, qyt, bx, bxt, pick, kind = call(
        functools.partial(species_kernel, **sizes),
        [same(sp3)] + [same(v) for v in consts],
        [spec_hbm()] * 9,
        [lines_v, compact_v, vmem(place_t.shape, jnp.int32), smem, padded_species]
        + [dma(9), dma(2), dma(2)],
        "species",
        52,
        5 * 10**9,
        out_specs=[spec_hbm()] + [spec_vmem()] * 6,
    )(*consts, lines, place, offset)

    me = lax.axis_index("gx") * nb + lax.axis_index("gy")
    lam_here = lax.dynamic_slice(jnp.asarray(tab["lamz"]), (me * modes,), (modes,))
    lam = tab["lamx"] + jnp.tile(lam_here, wx * na)[:, None]
    plane_rows = wx * na * modes
    back = pl.pallas_call(
        functools.partial(solve_kernel, na=na, nb=nb, wide=wy, keep=keep),
        out_shape=sds((devices, (keep + 1) * LANES), f32),
        in_specs=[spec_vmem()] * 9,
        out_specs=spec_vmem(),
        scratch_shapes=[
            pltpu.VMEM((plane_rows, wy * nb), f32),
            pltpu.VMEM((devices * keep, LANES), f32),
        ],
        compiler_params=params(12),
        name="solve",
    )(
        wave,
        lam,
        tab["lamy"],
        qy,
        qyt,
        bx,
        bxt,
        pick,
        kind,
    )

    inv = jnp.asarray(tab["inv"])
    species_out, inv = call(
        functools.partial(species_rest_kernel, **sizes),
        [same(sp3), same(inv)],
        [spec_any()] + [spec_hbm()] * 5,
        [lines_v, compact_v, vmem(place_t.shape, jnp.int32), smem, padded_species]
        + [dma(4), dma(2), dma(2)],
        "speciesrest",
        52,
        5 * 10**9,
        {1: 0},
        out_specs=[spec_hbm(), spec_vmem()],
    )(back, species_out, inv, lines, place, offset)

    back = lax.all_to_all(back, ("gx", "gy"), 0, 0, tiled=True)

    velocity_out = pl.pallas_call(
        functools.partial(slope_kernel, wx=wx, wy=wy, modes=modes),
        out_shape=sds((3 * rows, depth), f32),
        in_specs=[spec_vmem()] * 3,
        out_specs=spec_vmem(),
        scratch_shapes=[
            pltpu.VMEM((tab["inv"].shape[0], LANES), f32),
            pltpu.VMEM((modes, LANES, depth), f32),
            pltpu.VMEM((rows + wy, depth), f32),
        ],
        compiler_params=params(12),
        name="slope",
    )(back, inv, vel)
    return (species_out.reshape(species.shape), velocity_out.reshape(velocity.shape))


def solution(mesh):
    return jax.shard_map(
        per_device,
        mesh=mesh,
        in_specs=(
            P(None, "gx", "gy", None),
            P("gx", "gy", None),
            P(),
            P(None, "gx", "gy", None),
            P(),
            P(),
            P(),
            P(),
            P(),
            P("gx", "gy", None),
            P("gx", "gy"),
        ),
        out_specs=(P(None, "gx", "gy", None), P(None, "gx", "gy", None)),
        check_vma=False,
    )
```
